128 devices in a mesh: win: 8 (over y, core), blk: 16 (over z, x).
Axes of the slice: x: 4, y: 4, z: 4, core: 2. Of those that a mesh axis runs over, the one named last changes fastest.
Arguments:
- records: bfloat16 [32, 8192, 4096], P('win', 'blk'), may hold values from -6 to 6
- active: int32 [16, 5], P('blk'), may hold values from 0 to 1, as said below
Outputs:
- summary: bfloat16 [16, 5, 8, 1024, 512], P('blk', None, 'win')
The draws below stay inside these ranges and needn't reach their ends.
Inputs may be any that keep to these rules, and one draw needn't show every extreme that they name: active[a, s] is 1 or 0; it is 0 wherever a + s >= 16; active[a, 0] is 1 for every block; some block has all 5 entries 1.
All inputs are finite; a program needn't handle non-finite values.
Results may differ from the reference program's by a relative error of at most 0.0056.
Values may be sent and summed in bfloat16 or wider, within the bound.
A program may use at most 64 MiB of HBM per device.

```python
import math
import jax
import jax.numpy as jnp
from jax import lax

SAMPLES = 4096
BINS = 256
BIN0 = 16
BLOCK = 512
BANDS = 8
SLOTS = 5
WINDOWS = 32
BLOCKS = 16
STATIONS = 8192
BAND_BINS = 32


def draw_active(key, part):
    key = jax.random.fold_in(key, 7)
    key_full, key_coin = jax.random.split(key)
    owner_ids = jnp.arange(BLOCKS, dtype=jnp.int32)[:, None]
    slot_ids = jnp.arange(SLOTS, dtype=jnp.int32)[None, :]
    full_owner = jax.random.randint(key_full, (), 0, BLOCKS - SLOTS + 1)
    coin_draw = jax.random.randint(key_coin, (BLOCKS, SLOTS), 0, 3)
    kept_slots = (coin_draw == 0) | (slot_ids == 0) | (owner_ids == full_owner)
    inside = owner_ids + slot_ids < BLOCKS
    return (kept_slots & inside).astype(jnp.int32)


def block_scale(rng, shape, pieces, least, high):
    loudness, own = 1.0, jax.random.fold_in(rng, 6)
    for axis_at, parts in pieces:
        heights = jnp.exp(jax.random.uniform(jax.random.fold_in(own, axis_at), (parts,), jnp.float32, least / len(pieces), high / len(pieces)))
        loudness = loudness * jnp.repeat(heights, shape[axis_at] // parts).reshape([-1 if axis == axis_at else 1 for axis in range(len(shape))])
    return loudness


def centred(key, shape, width, limit, cuts=(), held_as=jnp.bfloat16):
    drawn = width * jax.random.normal(key, shape, jnp.float32)
    if cuts:
        drawn = drawn * block_scale(key, shape, cuts, -0.22, 0.18)
    return jnp.clip(drawn, -limit, limit).astype(held_as)


def setup_inputs(seed: int = 0) -> dict:
    seeds = jax.random.split(jax.random.key(seed), 3)
    return {
        "records": centred(seeds[0], (WINDOWS, STATIONS, SAMPLES), 1.0, 6.0, ((0, 8), (1, 16))),
        "active": draw_active(jax.random.fold_in(seeds[2], 71), 0),
    }


EPSILON = 1e-06

def spectral_table(samples, first_bin, num_bins):
    sample_idx = jnp.arange(samples, dtype=jnp.int32)[:, None]
    bin_idx = (jnp.arange(num_bins, dtype=jnp.int32) + first_bin)[None, :]
    phase_idx = sample_idx * bin_idx % samples
    angles = phase_idx.astype(jnp.float32) * (2.0 * math.pi / samples)
    return jnp.concatenate([jnp.cos(angles), -jnp.sin(angles)], axis=1).astype(jnp.bfloat16)

def band_matrix(whitened, block_idx, band_idx):
    block_slab = lax.dynamic_slice_in_dim(whitened, (block_idx * BLOCK).astype(jnp.int32), BLOCK, 1)
    lower = band_idx * BAND_BINS
    real_part = block_slab[:, :, lower:lower + BAND_BINS]
    imag_part = block_slab[:, :, BINS + lower:BINS + lower + BAND_BINS]
    stacked = jnp.concatenate([real_part, imag_part], axis=1)
    return jnp.transpose(stacked, (0, 2, 1)).reshape(-1, 2 * BLOCK)

def reference(records, active):
    basis_table = spectral_table(SAMPLES, BIN0, BINS)

    def one_window(window_rows):
        spectra = jnp.dot(window_rows, basis_table, preferred_element_type=jnp.float32)
        power_mean = lax.optimization_barrier(jnp.sum(spectra * spectra, axis=1, keepdims=True)) / BINS
        return (spectra * lax.rsqrt(power_mean + EPSILON)).astype(jnp.bfloat16)
    whitened = lax.map(one_window, records)
    inv_scale = 1.0 / math.sqrt(WINDOWS * BAND_BINS)

    def one_owner(owner_idx):
        slot_rows = []
        for slot_idx in range(SLOTS):
            partner_idx = jnp.minimum(owner_idx + slot_idx, BLOCKS - 1)
            factor = active[owner_idx, slot_idx].astype(jnp.float32) * inv_scale
            band_rows = []
            for band_idx in range(BANDS):
                left = band_matrix(whitened, owner_idx, band_idx)
                right = band_matrix(whitened, partner_idx, band_idx)
                products = jnp.dot(left.T, right, preferred_element_type=jnp.float32)
                real_sum = products[:BLOCK, :BLOCK] + products[BLOCK:, BLOCK:]
                imag_sum = products[BLOCK:, :BLOCK] - products[:BLOCK, BLOCK:]
                band_rows.append((jnp.concatenate([real_sum, imag_sum], axis=0) * factor).astype(jnp.bfloat16))
            slot_rows.append(jnp.stack(band_rows))
        return jnp.stack(slot_rows)
    return lax.map(one_owner, jnp.arange(BLOCKS, dtype=jnp.int32))
```

```python
import functools
import math

import jax
import jax.numpy as jnp
import ml_dtypes
import numpy as np
from jax import lax
from jax.experimental import pallas as pl
from jax.experimental.pallas import tpu as pltpu
from jax.sharding import PartitionSpec as P

SAMPLES = 4096
BINS = 256
BIN0 = 16
SLOTS = 5
BAND_BINS = 32
EPSILON = 1e-06

WIN = 8
RING = 4
BLOCKS = 16
LOCAL_W = 4
ST = 512
Q = 128
K = 1024
PIECES = 32
LAG = 3

MESH = pl.DeviceIdType.MESH
F32 = jnp.float32
BF16 = jnp.bfloat16

OWN, UP4, UP1, UP3 = 0, 1, 2, 3


def spectral_table():
    phase = (np.arange(BINS)[:, None] + BIN0) * np.arange(SAMPLES)[None, :] % SAMPLES
    angles = phase.astype(np.float32) * np.float32(2.0 * math.pi / SAMPLES)
    angles = angles.astype(np.float64)
    return np.concatenate([np.cos(angles), -np.sin(angles)]).astype(np.float32).astype(ml_dtypes.bfloat16)


def kernel(active, rec, table, out, tab, rbuf, wh, blk, a2, lt, rp, rv, ost,
           tab_sem, rec_sem, aa_send, aa_recv, z_send, z_recv, m_send, m_recv, p_send, p_recv,
           a2_send, a2_recv, ret_send, ret_recv, out_sem):
    me = lax.axis_index("win")
    b = lax.axis_index("blk")
    z, x = b // RING, b % RING

    def peer(i):
        return (lax.rem(me + i, WIN), b)

    def at(dz, dx):
        return (me, lax.rem(z + dz + RING, RING) * RING + lax.rem(x + dx + RING, RING))

    nxt = (me, lax.rem(b + 1, BLOCKS))
    prv = (me, lax.rem(b + BLOCKS - 1, BLOCKS))

    barrier = pltpu.get_barrier_semaphore()
    for i in range(1, WIN):
        pl.semaphore_signal(barrier, inc=1, device_id=peer(i), device_id_type=MESH)
    for dev in (at(-1, 0), at(1, 0), at(0, -1), at(0, 1), nxt, prv):
        pl.semaphore_signal(barrier, inc=1, device_id=dev, device_id_type=MESH)

    pltpu.make_async_copy(table, tab, tab_sem).start()
    for sc in range(8):
        h, w = sc // LOCAL_W, sc % LOCAL_W
        pltpu.make_async_copy(rec.at[w, pl.ds(h * 2 * Q, 2 * Q), :], rbuf.at[sc], rec_sem.at[sc]).start()

    pltpu.make_async_copy(table, tab, tab_sem).wait()
    pl.semaphore_wait(barrier, WIN - 1 + 6)

    def transform(sc):
        h, w = sc // LOCAL_W, sc % LOCAL_W
        pltpu.make_async_copy(rbuf.at[sc], rbuf.at[sc], rec_sem.at[sc]).wait()
        spectra = lax.dot_general(tab[...], rbuf[sc], (((1,), (1,)), ((), ())), preferred_element_type=F32)
        power = jnp.sum(spectra * spectra, axis=0, keepdims=True) / BINS
        white = (spectra * lax.rsqrt(power + EPSILON)).astype(BF16)
        for q in range(WIN):
            for ri in range(2):
                for qt in range(2):
                    wh[sc, q, qt, ri] = white[ri * BINS + q * BAND_BINS:ri * BINS + (q + 1) * BAND_BINS,
                                              qt * Q:(qt + 1) * Q]
        row = pl.multiple_of((w * WIN + me) * BAND_BINS, BAND_BINS)

        @pl.loop(1, WIN)
        def _(i):
            to = peer(i)
            pltpu.make_async_remote_copy(
                src_ref=wh.at[sc, to[0]],
                dst_ref=blk.at[OWN, pl.ds(h * 2, 2), :, pl.ds(row, BAND_BINS), :],
                send_sem=aa_send.at[sc], recv_sem=aa_recv.at[sc], device_id=to, device_id_type=MESH,
            ).start()

        for qt in range(2):
            for ri in range(2):
                blk[OWN, h * 2 + qt, ri, pl.ds(row, BAND_BINS), :] = wh[sc, me, qt, ri]

    def piece(block, j):
        return blk.at[block, j // 8, j % 2, pl.ds((j // 2) % 4 * 256, 256), :]

    m_src = jnp.where(x >= 1, OWN, UP4)
    p_src = jnp.where(x <= 2, UP4, OWN)

    def wait_bytes(ref, sem):
        pltpu.make_async_copy(ref, ref, sem).wait()

    def tick(k):
        if k < PIECES:
            if k % 2 == 0 and (k // 8) % 2 == 0:
                sc = k // 16 * 4 + (k // 2) % 4
                wait_bytes(wh.at[sc, pl.ds(0, WIN - 1)], aa_recv.at[sc])
            pltpu.make_async_remote_copy(
                src_ref=piece(OWN, k), dst_ref=piece(UP4, k),
                send_sem=z_send, recv_sem=z_recv.at[k], device_id=at(-1, 0), device_id_type=MESH).start()
        j = k - LAG
        if 0 <= j < PIECES:
            wait_bytes(piece(UP4, j), z_recv.at[j])
            pltpu.make_async_remote_copy(
                src_ref=piece(m_src, j), dst_ref=piece(UP1, j),
                send_sem=m_send, recv_sem=m_recv.at[j // 2], device_id=at(0, -1), device_id_type=MESH).start()
            if j < 24:
                pltpu.make_async_remote_copy(
                    src_ref=piece(p_src, j), dst_ref=piece(UP3, j),
                    send_sem=p_send, recv_sem=p_recv.at[j // 8], device_id=at(0, 1), device_id_type=MESH).start()

    def wait_m(quarter):
        for w in range(4):
            rows = blk.at[UP1, quarter, :, pl.ds(w * 256, 256), :]
            wait_bytes(rows, m_recv.at[quarter * 4 + w])

    def wait_p(quarter):
        wait_bytes(blk.at[UP3, quarter], p_recv.at[quarter])

    def turn(left, block, quarter):
        for ri in range(2):
            lt[left, ri, quarter * Q:(quarter + 1) * Q, :] = blk[block, quarter, ri].T

    def columns(block, quarters, ri):
        parts = [blk[block, q, ri] for q in quarters]
        return parts[0] if len(parts) == 1 else jnp.concatenate(parts, axis=1)

    def products(left, rows, re, im):
        lre, lim = lt[left, 0, rows, :], lt[left, 1, rows, :]
        dot = functools.partial(jnp.dot, preferred_element_type=F32)
        real = dot(lre, re) + dot(lim, im)
        imag = dot(lim, re) - dot(lre, im)
        return real, imag

    def factor(slot):
        return active[0, slot].astype(F32) * (1.0 / math.sqrt(K))

    def put_out(slot, rows, cols):
        pltpu.make_async_copy(ost.at[slot, :, rows, cols], out.at[slot, :, rows, cols], out_sem).start()

    def summary(slot, block, quarters):
        cols = pl.ds(quarters[0] * Q, len(quarters) * Q)
        scale = factor(slot)

        @pl.loop(0, 2)
        def _(half):
            rows = pl.ds(pl.multiple_of(half * 256, 256), 256)
            if block is None:
                re, im = a2[0], a2[1]
            else:
                re, im = columns(block, quarters, 0), columns(block, quarters, 1)
            real, imag = products(0, rows, re, im)
            ost[slot, 0, rows, cols] = (real * scale).astype(BF16)
            ost[slot, 1, rows, cols] = (imag * scale).astype(BF16)
            put_out(slot, rows, cols)

    def ret_copy(n, rows, cols):
        return pltpu.make_async_remote_copy(
            src_ref=rp.at[:, rows, cols], dst_ref=rv.at[:, rows, cols],
            send_sem=ret_send.at[n], recv_sem=ret_recv.at[n], device_id=nxt, device_id_type=MESH)

    def give_back(block, row_quarters, quarters):
        cols = pl.ds(quarters[0] * Q, len(quarters) * Q)
        rows = pl.ds(row_quarters[0] * Q, len(row_quarters) * Q)
        re, im = columns(block, quarters, 0), columns(block, quarters, 1)
        real, imag = products(1, rows, re, im)
        scale = 1.0 / math.sqrt(K)
        rp[0, rows, cols] = (real * scale).astype(BF16)
        rp[1, rows, cols] = (imag * scale).astype(BF16)

    def take_back(rows, cols, slot):
        flag = active[0, slot].astype(F32)
        ost[slot, :, rows, cols] = (rv[:, rows, cols].astype(F32) * flag).astype(BF16)
        put_out(slot, rows, cols)

    RETURNS = [
        (pl.ds(0, 256), pl.ds(0, 256)),
        (pl.ds(0, 256), pl.ds(256, 128)),
        (pl.ds(256, 128), pl.ds(0, 384)),
        (pl.ds(0, 384), pl.ds(384, 128)),
        (pl.ds(384, 128), pl.ds(0, 512)),
    ]

    def returned(n):
        ret_copy(n, *RETURNS[n]).start()

    def quantum(k):
        if k < 4:
            transform(k + 4)
        elif k == 10:
            turn(0, OWN, 0)
            turn(0, OWN, 1)
        elif k == 22:
            wait_m(0)
            wait_m(1)
            turn(1, UP1, 0)
            turn(1, UP1, 1)
        elif k == 23:
            wait_p(0)
            wait_p(1)
            give_back(UP3, (0, 1), (0, 1))
            returned(0)
        elif k == 24:
            turn(0, OWN, 2)
            turn(0, OWN, 3)
        elif k == 25:
            summary(0, OWN, (0, 1))
        elif k == 26:
            summary(0, OWN, (2, 3))
        elif k == 27:
            summary(4, UP4, (0, 1))
        elif k == 28:
            summary(1, UP1, (0, 1))
        elif k == 29:
            summary(3, UP3, (0, 1))
        elif k == 30:
            wait_p(2)
            give_back(UP3, (0, 1), (2,))
            returned(1)
        elif k == 31:
            wait_m(2)
            turn(1, UP1, 2)
            give_back(UP3, (2,), (0, 1))
            give_back(UP3, (2,), (2,))
            returned(2)
        elif k == 33:
            summary(3, UP3, (2,))

    @pl.loop(0, 4)
    def _(sc):
        transform(sc)

    for k in range(PIECES + LAG):
        tick(k)
        quantum(k)

    give_back(UP4, (0, 1, 2), (3,))
    returned(3)
    for w in range(4):
        rows = pl.ds(w * 256, 256)
        wait_bytes(blk.at[UP1, 3, :, rows, :], m_recv.at[12 + w])
        pltpu.make_async_remote_copy(
            src_ref=blk.at[UP1, 3, :, rows, :], dst_ref=a2.at[:, rows, :],
            send_sem=a2_send, recv_sem=a2_recv, device_id=prv, device_id_type=MESH).start()
    turn(1, UP1, 3)
    give_back(UP3, (3,), (0, 1))
    give_back(UP3, (3,), (2,))
    give_back(UP4, (3,), (3,))
    returned(4)
    summary(1, UP1, (2, 3))
    summary(4, UP4, (2, 3))

    for n in range(4):
        rows, cols = RETURNS[n]
        ret_copy(n, rows, cols).wait_recv()
        take_back(rows, cols, 3 if n == 3 else 2)
    wait_bytes(a2, a2_recv)
    summary(2, None, (3,))
    ret_copy(4, *RETURNS[4]).wait_recv()
    take_back(pl.ds(384, 128), pl.ds(0, 384), 2)
    take_back(pl.ds(384, 128), pl.ds(384, 128), 3)

    for n in range(5):
        ret_copy(n, *RETURNS[n]).wait_send()
    wait_bytes(a2, a2_send)
    wait_bytes(blk.at[OWN], z_send)
    wait_bytes(blk.at[OWN], m_send)
    wait_bytes(blk.at[OWN, pl.ds(0, 3)], p_send)
    for sc in range(8):
        wait_bytes(wh.at[sc, pl.ds(0, WIN - 1)], aa_send.at[sc])
    pltpu.make_async_copy(ost, out, out_sem).wait()


def shards(records, active):
    dma = pltpu.SemaphoreType.DMA
    out = pl.pallas_call(
        kernel,
        out_shape=jax.ShapeDtypeStruct((SLOTS, 2, ST, ST), BF16),
        in_specs=[
            pl.BlockSpec(memory_space=pltpu.SMEM),
            pl.BlockSpec(memory_space=pl.ANY),
            pl.BlockSpec(memory_space=pl.ANY),
        ],
        out_specs=pl.BlockSpec(memory_space=pl.ANY),
        scratch_shapes=[
            pltpu.VMEM((2 * BINS, SAMPLES), BF16),
            pltpu.VMEM((8, 2 * Q, SAMPLES), BF16),
            pltpu.VMEM((8, WIN, 2, 2, BAND_BINS, Q), BF16),
            pltpu.VMEM((4, 4, 2, K, Q), BF16),
            pltpu.VMEM((2, K, Q), BF16),
            pltpu.VMEM((2, 2, ST, K), BF16),
            pltpu.VMEM((2, ST, ST), BF16),
            pltpu.VMEM((2, ST, ST), BF16),
            pltpu.VMEM((SLOTS, 2, ST, ST), BF16),
            dma, dma((8,)), dma((8,)), dma((8,)), dma, dma((PIECES,)), dma, dma((16,)), dma, dma((3,)),
            dma, dma, dma((5,)), dma((5,)), dma,
        ],
        compiler_params=pltpu.CompilerParams(
            collective_id=0, has_side_effects=True, vmem_limit_bytes=60 * 2**20),
        cost_estimate=pl.CostEstimate(flops=20 * 2**30, bytes_accessed=25 * 2**20, transcendentals=0),
    )(active, records, jnp.asarray(spectral_table()))
    return out.reshape(1, SLOTS, 1, 2 * ST, ST)


def solution(mesh):
    return jax.shard_map(
        shards,
        mesh=mesh,
        in_specs=(P("win", "blk", None), P("blk", None)),
        out_specs=P("blk", None, "win", None, None),
        check_vma=False,
    )
```

```python
import functools
import math

import jax
import jax.numpy as jnp
import ml_dtypes
import numpy as np
from jax import lax
from jax.experimental import pallas as pl
from jax.experimental.pallas import tpu as pltpu
from jax.sharding import PartitionSpec as P

SAMPLES = 4096
BINS = 256
BIN0 = 16
SLOTS = 5
BAND_BINS = 32
EPSILON = 1e-06

WIN = 8
RING = 4
BLOCKS = 16
LOCAL_W = 4
ST = 512
Q = 128
K = 1024
PIECES = 32
SLOTS_IN = 4

MESH = pl.DeviceIdType.MESH
F32 = jnp.float32
BF16 = jnp.bfloat16

OWN, UP4, UP1, UP3 = 0, 1, 2, 3


def spectral_table():
    phase = (np.arange(BINS)[:, None] + BIN0) * np.arange(SAMPLES)[None, :] % SAMPLES
    angles = phase.astype(np.float32) * np.float32(2.0 * math.pi / SAMPLES)
    angles = angles.astype(np.float64)
    return np.concatenate([np.cos(angles), -np.sin(angles)]).astype(np.float32).astype(ml_dtypes.bfloat16)


def pick(step, table, default=-1):
    value = jnp.int32(default)
    for at_step, entry in table.items():
        value = jnp.where(step == at_step, jnp.int32(entry), value)
    return value


START = 4
AHEAD = 3
TRANSFORM = {1: 1, 3: 2, 6: 3, 10: 4, 13: 5, 15: 6, 17: 7}
SPREAD = {2: 1, 5: 2, 6: 3, 10: 4, 13: 5, 15: 6, 17: 7}
GATHERED = {5: 1, 9: 2, 13: 3, 17: 4, 19: 5, 21: 6, 23: 7}
WAIT_M = {24: (0, 2), 30: (2, 3)}
WAIT_P = {25: (0, 2), 30: (2, 3)}
TURN = {13: (0, 0, 2), 23: (0, 2, 4), 24: (1, 0, 2), 30: (1, 2, 3), 37: (1, 3, 4)}
TILES = {25: (0, 2), 26: (2, 4), 30: (4, 6), 31: (6, 9), 35: (9, 12), 37: (12, 14), 38: (14, 16)}
RETURN = {28: (0,), 31: (1, 2), 35: (3,), 38: (4,)}
SUMMARY = {14: (0, 0, 0), 20: (4, 0, 0), 27: (1, 0, 0), 28: (3, 0, 0), 29: (0, 0, 1), 32: (0, 1, 0), 33: (0, 1, 1),
           34: (4, 1, 0), 36: (3, 1, 0), 39: (1, 1, 0), 40: (4, 0, 1), 41: (4, 1, 1), 42: (1, 0, 1), 43: (1, 1, 1)}
NARROW = {44: 2}
PART = {45: 0, 46: 1, 47: 2, 49: 3}
FORWARD = {35: (0, 2), 37: (2, 4)}
TAKE = {39: (0,), 45: (1, 2), 46: (3,), 48: (4,)}
STEPS = 50
TILE_AT = [(0, 0), (0, 1), (1, 0), (1, 1), (0, 2), (1, 2), (2, 0), (2, 1), (2, 2),
           (0, 3), (1, 3), (2, 3), (3, 0), (3, 1), (3, 2), (3, 3)]
TILES_OF = [(0, 4), (4, 6), (6, 9), (9, 12), (12, 16)]


def kernel(active_in, rec, table, out, active, tab, rbuf, wh, blk, lt, rp, rv, ost, acc,
           tab_sem, rec_sem, aa_send, aa_recv, z_send, z_recv, m_send, m_recv, p_send, p_recv,
           a2_send, a2_recv, ret_send, ret_recv, out_sem, active_sem):
    me = lax.axis_index("win")
    b = lax.axis_index("blk")
    z, x = b // RING, b % RING

    def peer(i):
        return (lax.rem(me + i, WIN), b)

    def at(dz, dx):
        return (me, lax.rem(z + dz + RING, RING) * RING + lax.rem(x + dx + RING, RING))

    nxt = (me, lax.rem(b + 1, BLOCKS))
    prv = (me, lax.rem(b + BLOCKS - 1, BLOCKS))

    def load(sc):
        slot = sc % SLOTS_IN
        return pltpu.make_async_copy(
            rec.at[sc % LOCAL_W, pl.ds(pl.multiple_of(sc // LOCAL_W * 2 * Q, 2 * Q), 2 * Q), :],
            rbuf.at[slot], rec_sem.at[slot])

    fetch = pltpu.make_async_copy(table, tab, tab_sem)
    fetch.start()
    load(0).start()
    flags = pltpu.make_async_copy(active_in, active, active_sem)
    flags.start()

    barrier = pltpu.get_barrier_semaphore()
    for i in range(1, WIN):
        pl.semaphore_signal(barrier, inc=1, device_id=peer(i), device_id_type=MESH)
    for dev in (at(-1, 0), at(1, 0), at(0, -1), at(0, 1), nxt, prv):
        pl.semaphore_signal(barrier, inc=1, device_id=dev, device_id_type=MESH)

    def transform(sc):
        load(sc).wait()
        spectra = lax.dot_general(
            tab[...], rbuf[sc % SLOTS_IN], (((1,), (1,)), ((), ())), preferred_element_type=F32)
        power = jnp.sum(spectra * spectra, axis=0, keepdims=True) / BINS
        white = (spectra * lax.rsqrt(power + EPSILON)).astype(BF16)
        for q in range(WIN):
            for ri in range(2):
                for qt in range(2):
                    wh[sc, q, qt, ri] = white[ri * BINS + q * BAND_BINS:ri * BINS + (q + 1) * BAND_BINS,
                                              qt * Q:(qt + 1) * Q]

        if isinstance(sc, int):
            load(sc + SLOTS_IN).start()
        else:
            @pl.when(sc + SLOTS_IN < 8)
            def _():
                load(sc + SLOTS_IN).start()

    def spread(sc, quarters, recv):
        h, w = sc // LOCAL_W, sc % LOCAL_W
        row = pl.multiple_of((w * WIN + me) * BAND_BINS, BAND_BINS)

        @pl.loop(1, WIN)
        def _(i):
            to = peer(i)
            pltpu.make_async_remote_copy(
                src_ref=wh.at[sc, to[0], quarters],
                dst_ref=blk.at[OWN, pl.ds(h * 2 + quarters.start, quarters.size), :, pl.ds(row, BAND_BINS), :],
                send_sem=aa_send.at[sc], recv_sem=aa_recv.at[recv], device_id=to, device_id_type=MESH,
            ).start()

        for qt in range(quarters.start, quarters.start + quarters.size):
            for ri in range(2):
                blk[OWN, h * 2 + qt, ri, pl.ds(row, BAND_BINS), :] = wh[sc, me, qt, ri]

    def place(j):
        early = j < 16
        return jnp.where(early, j // 2 % 2, j // 8), jnp.where(early, j // 4, j // 2 % 4)

    def piece(block, j):
        quarter, w = place(j)
        return blk.at[block, quarter, j % 2, pl.ds(pl.multiple_of(w * 256, 256), 256), :]

    def wait_bytes(ref, sem):
        pltpu.make_async_copy(ref, ref, sem).wait()

    def send_z(j):
        pltpu.make_async_remote_copy(
            src_ref=piece(OWN, j), dst_ref=piece(UP4, j),
            send_sem=z_send, recv_sem=z_recv.at[j], device_id=at(-1, 0), device_id_type=MESH).start()

    def send_m(block, j):
        quarter, w = place(j)
        pltpu.make_async_remote_copy(
            src_ref=piece(block, j), dst_ref=piece(UP1, j),
            send_sem=m_send, recv_sem=m_recv.at[quarter * 4 + w], device_id=at(0, -1), device_id_type=MESH).start()

    def send_p(block, j):
        quarter, _ = place(j)
        pltpu.make_async_remote_copy(
            src_ref=piece(block, j), dst_ref=piece(UP3, j),
            send_sem=p_send, recv_sem=p_recv.at[quarter], device_id=at(0, 1), device_id_type=MESH).start()

    def turn(left, quarter):
        block = jnp.where(left == 0, OWN, UP1)
        for ri in range(2):
            lt[left, ri, pl.ds(pl.multiple_of(quarter * Q, Q), Q), :] = blk[block, quarter, ri].T

    def products(left, rows, re, im, window=slice(None)):
        lre, lim = lt[left, 0, rows, window], lt[left, 1, rows, window]
        dot = functools.partial(jnp.dot, preferred_element_type=F32)
        real = dot(lre, re) + dot(lim, im)
        imag = dot(lim, re) - dot(lre, im)
        return real, imag

    def put_out(slot, rows, cols):
        pltpu.make_async_copy(ost.at[slot, :, rows, cols], out.at[slot, :, rows, cols], out_sem).start()

    def summary(slot, block, quarter, width, first, last):
        cols = pl.ds(pl.multiple_of(quarter * Q, Q), width * Q)
        scale = active[0, slot].astype(F32) * (1.0 / math.sqrt(K))

        @pl.loop(first, last)
        def _(half):
            rows = pl.ds(pl.multiple_of(half * 256, 256), 256)
            re = jnp.concatenate([blk[block, quarter + i, 0] for i in range(width)], axis=1)
            im = jnp.concatenate([blk[block, quarter + i, 1] for i in range(width)], axis=1)
            real, imag = products(0, rows, re, im)
            ost[slot, 0, rows, cols] = (real * scale).astype(BF16)
            ost[slot, 1, rows, cols] = (imag * scale).astype(BF16)
            put_out(slot, rows, cols)

    def part(w):
        window = pl.ds(pl.multiple_of(w * 256, 256), 256)
        wait_bytes(blk.at[UP3, 3, :, window, :], a2_recv.at[w])
        scale = active[0, 2].astype(F32) * (1.0 / math.sqrt(K))

        @pl.loop(0, 2)
        def _(half):
            rows = pl.ds(pl.multiple_of(half * 256, 256), 256)
            real, imag = products(0, rows, blk[UP3, 3, 0, window, :], blk[UP3, 3, 1, window, :], window)
            acc[0, rows, :] += real
            acc[1, rows, :] += imag

            @pl.when(w == 3)
            def _():
                cols = pl.ds(3 * Q, Q)
                ost[2, :, rows, cols] = (acc[:, rows, :] * scale).astype(BF16)
                put_out(2, rows, cols)

    def tile_at(n):
        return (pick(n, {i: rc[0] for i, rc in enumerate(TILE_AT)}, 0),
                pick(n, {i: rc[1] for i, rc in enumerate(TILE_AT)}, 0))

    def ret_copy(n):
        sl = [
            (pl.ds(0, 2), slice(None), pl.ds(0, 256)),
            (pl.ds(2, 1), slice(None), pl.ds(0, 256)),
            (pl.ds(0, 3), slice(None), pl.ds(256, 128)),
            (pl.ds(3, 1), slice(None), pl.ds(0, 384)),
            (pl.ds(0, 4), slice(None), pl.ds(384, 128)),
        ][n]
        return pltpu.make_async_remote_copy(
            src_ref=rp.at[sl], dst_ref=rv.at[sl],
            send_sem=ret_send.at[n], recv_sem=ret_recv.at[n], device_id=nxt, device_id_type=MESH)

    def give_back(n):
        r, c = tile_at(n)
        rows = pl.ds(pl.multiple_of(r * Q, Q), Q)
        block = jnp.where(c == 3, UP4, UP3)
        real, imag = products(1, rows, blk[block, c, 0], blk[block, c, 1])
        scale = 1.0 / math.sqrt(K)
        rp[c, 0, rows, :] = (real * scale).astype(BF16)
        rp[c, 1, rows, :] = (imag * scale).astype(BF16)

    def take_back(n):
        r, c = tile_at(n)
        rows, cols = pl.ds(pl.multiple_of(r * Q, Q), Q), pl.ds(pl.multiple_of(c * Q, Q), Q)
        slot = jnp.where(c == 3, 3, 2)
        flag = active[0, slot].astype(F32)
        ost[slot, :, rows, cols] = (rv[c, :, rows, :].astype(F32) * flag).astype(BF16)
        put_out(slot, rows, cols)

    def when_in(step, table):
        def run(body):
            entries = {k: v if isinstance(v, tuple) else (v,) for k, v in table.items()}
            first = pick(step, {k: v[0] for k, v in entries.items()})

            @pl.when(first >= 0)
            def _():
                rest = [pick(step, {k: v[i] for k, v in entries.items()}, 0)
                        for i in range(1, len(next(iter(entries.values()))))]
                body(first, *rest)
        return run

    fetch.wait()
    flags.wait()
    for sc in range(1, SLOTS_IN):
        load(sc).start()
    transform(0)
    pl.semaphore_wait(barrier, WIN - 1 + 6)
    spread(0, pl.ds(0, 1), 0)
    spread(0, pl.ds(1, 1), 8)
    acc[...] = jnp.zeros_like(acc)

    @pl.loop(1, STEPS)
    def _(step):
        k = step - START

        @pl.when((k >= 0) & (k < PIECES))
        def _():
            wait_bytes(piece(UP4, k), z_recv.at[k])

            @pl.when((x <= 2) & (k < 24))
            def _():
                send_p(UP4, k)

            @pl.when(x == 0)
            def _():
                send_m(UP4, k)

        @when_in(step, {START - 2: 0, START - 1: 8})
        def _(recv):
            wait_bytes(wh.at[0, pl.ds(0, WIN - 1), 0], aa_recv.at[recv])

        @when_in(step, GATHERED)
        def _(sc):
            wait_bytes(wh.at[sc, pl.ds(0, WIN - 1)], aa_recv.at[sc])

        lo = jnp.where(k < 0, 2 * (k + 2), k + AHEAD)
        hi = jnp.where(k < 0, jnp.maximum(lo, 0) + jnp.where(k >= -2, 2, 0), jnp.where(k >= 1, jnp.minimum(k + 1 + AHEAD, PIECES), 0))
        lo = jnp.maximum(lo, 0)

        @pl.loop(lo, hi)
        def _(j):
            send_z(j)

            @pl.when(x >= 1)
            def _():
                send_m(OWN, j)

            @pl.when((x == 3) & (j < 24))
            def _():
                send_p(OWN, j)

        @when_in(step, FORWARD)
        def _(first, last):
            @pl.loop(first, last)
            def _(w):
                rows = pl.ds(pl.multiple_of(w * 256, 256), 256)
                wait_bytes(blk.at[UP1, 3, :, rows, :], m_recv.at[12 + w])
                pltpu.make_async_remote_copy(
                    src_ref=blk.at[UP1, 3, :, rows, :], dst_ref=blk.at[UP3, 3, :, rows, :],
                    send_sem=a2_send, recv_sem=a2_recv.at[w], device_id=prv, device_id_type=MESH).start()

        @when_in(step, TRANSFORM)
        def _(sc):
            transform(sc)

        @when_in(step, SPREAD)
        def _(sc):
            spread(sc, pl.ds(0, 2), sc)

        @when_in(step, WAIT_M)
        def _(first, last):
            @pl.loop(first * 4, last * 4)
            def _(i):
                rows = pl.ds(pl.multiple_of(i % 4 * 256, 256), 256)
                wait_bytes(blk.at[UP1, i // 4, :, rows, :], m_recv.at[i])

        @when_in(step, WAIT_P)
        def _(first, last):
            @pl.loop(first, last)
            def _(quarter):
                wait_bytes(blk.at[UP3, quarter], p_recv.at[quarter])

        @when_in(step, TURN)
        def _(left, first, last):
            @pl.loop(first, last)
            def _(quarter):
                turn(left, quarter)

        @when_in(step, TILES)
        def _(first, last):
            @pl.loop(first, last)
            def _(n):
                give_back(n)

        for at_step, ns in RETURN.items():
            @pl.when(step == at_step)
            def _():
                for n in ns:
                    ret_copy(n).start()

        @when_in(step, SUMMARY)
        def _(slot, half, pair):
            block = pick(slot, {0: OWN, 1: UP1, 3: UP3, 4: UP4}, 0)
            summary(slot, block, pair * 2, 2, half, half + 1)

        @when_in(step, NARROW)
        def _(quarter):
            summary(3, UP3, quarter, 1, 0, 2)

        @when_in(step, PART)
        def _(w):
            part(w)

        for at_step, ns in TAKE.items():
            @pl.when(step == at_step)
            def _():
                for n in ns:
                    ret_copy(n).wait_recv()

        tiles = {k: (TILES_OF[ns[0]][0], TILES_OF[ns[-1]][1]) for k, ns in TAKE.items()}

        @when_in(step, tiles)
        def _(first, last):
            @pl.loop(first, last)
            def _(n):
                take_back(n)

    for n in range(5):
        ret_copy(n).wait_send()
    wait_bytes(blk.at[UP3, 3], a2_send)
    wait_bytes(blk.at[OWN], z_send)
    wait_bytes(blk.at[OWN], m_send)
    wait_bytes(blk.at[OWN, pl.ds(0, 3)], p_send)
    for sc in range(8):
        wait_bytes(wh.at[sc, pl.ds(0, WIN - 1)], aa_send.at[sc])
    pltpu.make_async_copy(ost, out, out_sem).wait()


def shards(records, active):
    dma = pltpu.SemaphoreType.DMA
    out = pl.pallas_call(
        kernel,
        out_shape=jax.ShapeDtypeStruct((SLOTS, 2, ST, ST), BF16),
        in_specs=[
            pl.BlockSpec(memory_space=pltpu.HBM),
            pl.BlockSpec(memory_space=pltpu.HBM),
            pl.BlockSpec(memory_space=pltpu.HBM),
        ],
        out_specs=pl.BlockSpec(memory_space=pl.ANY),
        scratch_shapes=[
            pltpu.SMEM((1, SLOTS), jnp.int32),
            pltpu.VMEM((2 * BINS, SAMPLES), BF16),
            pltpu.VMEM((SLOTS_IN, 2 * Q, SAMPLES), BF16),
            pltpu.VMEM((8, WIN, 2, 2, BAND_BINS, Q), BF16),
            pltpu.VMEM((4, 4, 2, K, Q), BF16),
            pltpu.VMEM((2, 2, ST, K), BF16),
            pltpu.VMEM((4, 2, ST, Q), BF16),
            pltpu.VMEM((4, 2, ST, Q), BF16),
            pltpu.VMEM((SLOTS, 2, ST, ST), BF16),
            pltpu.VMEM((2, ST, Q), F32),
            dma, dma((SLOTS_IN,)), dma((8,)), dma((9,)), dma, dma((PIECES,)), dma, dma((16,)), dma, dma((3,)),
            dma, dma((4,)), dma((5,)), dma((5,)), dma, dma,
        ],
        compiler_params=pltpu.CompilerParams(
            collective_id=0, has_side_effects=True, vmem_limit_bytes=42 * 2**20),
        cost_estimate=pl.CostEstimate(flops=20 * 2**30, bytes_accessed=25 * 2**20, transcendentals=0),
    )(pltpu.with_memory_space_constraint(active, pltpu.HBM), records, pltpu.with_memory_space_constraint(jnp.asarray(spectral_table()), pltpu.HBM))
    return out.reshape(1, SLOTS, 1, 2 * ST, ST)


def solution(mesh):
    return jax.shard_map(
        shards,
        mesh=mesh,
        in_specs=(P("win", "blk", None), P("blk", None)),
        out_specs=P("blk", None, "win", None, None),
        check_vma=False,
    )
```

```python
import functools
import math

import jax
import jax.numpy as jnp
import ml_dtypes
import numpy as np
from jax import lax
from jax.experimental import pallas as pl
from jax.experimental.pallas import tpu as pltpu
from jax.sharding import PartitionSpec as P

SAMPLES = 4096
BINS = 256
BIN0 = 16
SLOTS = 5
BAND_BINS = 32
EPSILON = 1e-06

WIN = 8
RING = 4
BLOCKS = 16
LOCAL_W = 4
ST = 512
Q = 128
K = 1024
PIECES = 32
SLOTS_IN = 4

MESH = pl.DeviceIdType.MESH
F32 = jnp.float32
BF16 = jnp.bfloat16

OWN, UP4, UP1, UP3 = 0, 1, 2, 3


def spectral_table():
    phase = (np.arange(BINS)[:, None] + BIN0) * np.arange(HALF)[None, :] % SAMPLES
    angles = phase.astype(np.float32) * np.float32(2.0 * math.pi / SAMPLES)
    angles = angles.astype(np.float64)
    return np.concatenate([np.cos(angles), -np.sin(angles)]).astype(np.float32).astype(ml_dtypes.bfloat16)


def pick(k, table, default=-1):
    value = jnp.int32(default)
    for at_k, entry in table.items():
        value = jnp.where(k == at_k, jnp.int32(entry), value)
    return value


FIRST_STEP, LAST_STEP = -5, 43
HALF = SAMPLES // 2
PART_COLS = HALF // 4
AHEAD = 3
MORE_AHEAD = 8
FIRST = 8
TRANSFORM = {-5: 1, -1: 2, 2: 3, 6: 4, 9: 5, 11: 6, 13: 7}
SPREAD = {-4: 1, 1: 2, 2: 3, 6: 4, 9: 5, 11: 6, 13: 7}
GATHERED = {1: 1, 5: 2, 8: 3, 12: 4, 14: 5, 16: 6, 18: 7}
WAIT_M = {20: (0, 2), 26: (2, 3)}
WAIT_P = {21: (0, 2), 26: (2, 3)}
TURN = {9: (0, 0, 2), 19: (0, 2, 4), 20: (1, 0, 2), 26: (1, 2, 3), 33: (1, 3, 4)}
BACK_HALF = {21: 0}
BACK_TALL = {27: 2, 31: 3}
BACK_WIDE = {26: (2, 0), 33: (3, 0), 34: (3, 1)}
RETURN = {24: (0,), 27: (1, 2), 31: (3,), 34: (4,)}
RETURN_EARLY = 21
SUMMARY = {10: (0, 0, 0), 16: (4, 0, 0), 22: (1, 0, 0), 23: (3, 0, 0), 24: (0, 0, 1), 25: (0, 1, 0), 28: (0, 1, 1),
           29: (4, 1, 0), 30: (3, 1, 0), 32: (1, 1, 0), 35: (4, 0, 1), 36: (4, 1, 1), 37: (1, 0, 1), 38: (1, 1, 1)}
PART = {39: 0, 40: 1, 41: 2, 42: 3}
FORWARD = {33: (0, 4)}
TAKE = {31: (0,), 39: (1, 2), 41: (3,), 43: (4,)}
TILE_AT = [(0, 0), (0, 1), (1, 0), (1, 1), (0, 2), (1, 2), (2, 2), (2, 0), (2, 1),
           (0, 3), (1, 3), (2, 3), (3, 0), (3, 1), (3, 2), (3, 3)]
TILES_OF = [(0, 4), (4, 7), (7, 9), (9, 12), (12, 16)]


def kernel(active_in, rec, table, out, active, tab, rbuf, wh, blk, lt, rp, rv, ost, acc,
           tab_sem, first_sem, later_sem, rec_sem, aa_send, aa_recv, z_send, z_recv, m_send, m_recv, p_send, p_recv,
           a2_send, a2_recv, ret_send, ret_recv, out_sem, active_sem):
    me = lax.axis_index("win")
    b = lax.axis_index("blk")
    z, x = b // RING, b % RING

    def peer(i):
        return (lax.rem(me + i, WIN), b)

    def at(dz, dx):
        return (me, lax.rem(z + dz + RING, RING) * RING + lax.rem(x + dx + RING, RING))

    nxt = (me, lax.rem(b + 1, BLOCKS))
    prv = (me, lax.rem(b + BLOCKS - 1, BLOCKS))

    def load(sc):
        slot = sc % SLOTS_IN
        return pltpu.make_async_copy(
            rec.at[sc % LOCAL_W, pl.ds(pl.multiple_of(sc // LOCAL_W * 2 * Q, 2 * Q), 2 * Q), :],
            rbuf.at[slot], rec_sem.at[slot])

    def fetch(part):
        cols = pl.ds(pl.multiple_of(part * PART_COLS, PART_COLS), PART_COLS)
        later = pl.ds(pl.multiple_of(HALF + part * PART_COLS, PART_COLS), PART_COLS)
        return (pltpu.make_async_copy(table.at[:, cols], tab.at[:, cols], tab_sem.at[part]),
                pltpu.make_async_copy(rec.at[0, pl.ds(0, 2 * Q), cols], rbuf.at[0, :, cols], first_sem.at[part]),
                pltpu.make_async_copy(rec.at[0, pl.ds(0, 2 * Q), later], rbuf.at[0, :, later], later_sem.at[part]))

    for part in range(4):
        for copy in fetch(part):
            copy.start()
    flags = pltpu.make_async_copy(active_in, active, active_sem)
    flags.start()

    barrier = pltpu.get_barrier_semaphore()
    for i in range(1, WIN):
        pl.semaphore_signal(barrier, inc=1, device_id=peer(i), device_id_type=MESH)
    for dev in (at(-1, 0), at(1, 0), at(0, -1), at(0, 1), nxt, prv):
        pl.semaphore_signal(barrier, inc=1, device_id=dev, device_id_type=MESH)

    def against(table_rows, rows):
        return lax.dot_general(table_rows, rows, (((1,), (1,)), ((), ())), preferred_element_type=F32)

    def transform(sc):
        load(sc).wait()
        slot = sc % SLOTS_IN
        whiten(sc, against(tab[...], rbuf[slot, :, pl.ds(0, HALF)]), against(tab[...], rbuf[slot, :, pl.ds(HALF, HALF)]))

    def first_transform():
        acc[...] = jnp.zeros_like(acc)

        @pl.loop(0, 4)
        def _(part):
            for copy in fetch(part):
                copy.wait()
            cols = pl.ds(pl.multiple_of(part * PART_COLS, PART_COLS), PART_COLS)
            later = pl.ds(pl.multiple_of(HALF + part * PART_COLS, PART_COLS), PART_COLS)
            acc[0] += against(tab[:, cols], rbuf[0, :, cols])
            acc[1] += against(tab[:, cols], rbuf[0, :, later])

        for sc in range(1, SLOTS_IN):
            load(sc).start()
        whiten(0, acc[0], acc[1])

    def whiten(sc, early, later):
        odd = lax.broadcasted_iota(jnp.int32, early.shape, 0) % 2 == 1
        spectra = early + jnp.where(odd, -later, later)
        power = jnp.sum(spectra * spectra, axis=0, keepdims=True) / BINS
        white = (spectra * lax.rsqrt(power + EPSILON)).astype(BF16)
        for q in range(WIN):
            for ri in range(2):
                for qt in range(2):
                    wh[sc, q, qt, ri] = white[ri * BINS + q * BAND_BINS:ri * BINS + (q + 1) * BAND_BINS,
                                              qt * Q:(qt + 1) * Q]

        if isinstance(sc, int):
            load(sc + SLOTS_IN).start()
        else:
            @pl.when(sc + SLOTS_IN < 8)
            def _():
                load(sc + SLOTS_IN).start()

    def spread(sc, part=None):
        h, w = sc // LOCAL_W, sc % LOCAL_W
        row = pl.multiple_of((w * WIN + me) * BAND_BINS, BAND_BINS)

        @pl.loop(1, WIN)
        def _(i):
            to = peer(i)
            if part is None:
                src = wh.at[sc, to[0]]
                dst = blk.at[OWN, pl.ds(h * 2, 2), :, pl.ds(row, BAND_BINS), :]
            else:
                src = wh.at[sc, to[0], part // 2, part % 2]
                dst = blk.at[OWN, part // 2, part % 2, pl.ds(row, BAND_BINS), :]
            pltpu.make_async_remote_copy(
                src_ref=src, dst_ref=dst, send_sem=aa_send.at[sc],
                recv_sem=aa_recv.at[sc if part is None else FIRST + part],
                device_id=to, device_id_type=MESH,
            ).start()

        for own in range(4) if part is None else (part,):
            blk[OWN, h * 2 + own // 2, own % 2, pl.ds(row, BAND_BINS), :] = wh[sc, me, own // 2, own % 2]

    def place(j):
        early = j < 16
        return jnp.where(early, j // 2 % 2, j // 8), jnp.where(early, j // 4, j // 2 % 4)

    def piece(block, j):
        quarter, w = place(j)
        return blk.at[block, quarter, j % 2, pl.ds(pl.multiple_of(w * 256, 256), 256), :]

    def wait_bytes(ref, sem):
        pltpu.make_async_copy(ref, ref, sem).wait()

    def send_z(j):
        pltpu.make_async_remote_copy(
            src_ref=piece(OWN, j), dst_ref=piece(UP4, j),
            send_sem=z_send, recv_sem=z_recv.at[j], device_id=at(-1, 0), device_id_type=MESH).start()

    def send_m(block, j):
        quarter, w = place(j)
        pltpu.make_async_remote_copy(
            src_ref=piece(block, j), dst_ref=piece(UP1, j),
            send_sem=m_send, recv_sem=m_recv.at[quarter * 4 + w], device_id=at(0, -1), device_id_type=MESH).start()

    def send_p(block, j):
        quarter, _ = place(j)
        pltpu.make_async_remote_copy(
            src_ref=piece(block, j), dst_ref=piece(UP3, j),
            send_sem=p_send, recv_sem=p_recv.at[quarter], device_id=at(0, 1), device_id_type=MESH).start()

    def turn(left, quarter):
        block = jnp.where(left == 0, OWN, UP1)
        for ri in range(2):
            lt[left, ri, pl.ds(pl.multiple_of(quarter * Q, Q), Q), :] = blk[block, quarter, ri].T

    def products(left, rows, re, im, window=slice(None)):
        lre, lim = lt[left, 0, rows, window], lt[left, 1, rows, window]
        dot = functools.partial(jnp.dot, preferred_element_type=F32)
        real = dot(lre, re) + dot(lim, im)
        imag = dot(lim, re) - dot(lre, im)
        return real, imag

    def put_out(slot, rows, cols):
        pltpu.make_async_copy(ost.at[slot, :, rows, cols], out.at[slot, :, rows, cols], out_sem).start()

    def summary(slot, block, half, pair):
        rows = pl.ds(pl.multiple_of(half * 256, 256), 256)
        cols = pl.ds(pl.multiple_of(pair * 256, 256), 256)
        scale = active[0, slot].astype(F32) * (1.0 / math.sqrt(K))
        re, im = [jnp.concatenate([blk[block, pair * 2 + i, ri] for i in range(2)], axis=1) for ri in range(2)]
        real, imag = products(0, rows, re, im)
        ost[slot, 0, rows, cols] = (real * scale).astype(BF16)
        ost[slot, 1, rows, cols] = (imag * scale).astype(BF16)
        put_out(slot, rows, cols)

    def add_windows(w):
        window = pl.ds(pl.multiple_of(w * 256, 256), 256)
        wait_bytes(blk.at[UP3, 3, :, window, :], a2_recv.at[w])

        @pl.loop(0, 2)
        def _(half):
            rows = pl.ds(pl.multiple_of(half * 256, 256), 256)
            re, im = [jnp.concatenate([blk[UP3, c, ri, window, :] for c in (2, 3)], axis=1) for ri in range(2)]
            real, imag = products(0, rows, re, im, window)
            acc[0, rows, :] += real
            acc[1, rows, :] += imag

            @pl.when(w == 3)
            def _():
                for slot, c in ((3, 2), (2, 3)):
                    scale = active[0, slot].astype(F32) * (1.0 / math.sqrt(K))
                    cols = pl.ds(c * Q, Q)
                    ost[slot, :, rows, cols] = (acc[:, rows, (c - 2) * Q:(c - 1) * Q] * scale).astype(BF16)
                    put_out(slot, rows, cols)

    def tile_at(n):
        return (pick(n, {i: rc[0] for i, rc in enumerate(TILE_AT)}, 0),
                pick(n, {i: rc[1] for i, rc in enumerate(TILE_AT)}, 0))

    def ret_copy(n):
        sl = [
            (pl.ds(0, 2), slice(None), pl.ds(0, 256)),
            (pl.ds(2, 1), slice(None), pl.ds(0, 384)),
            (pl.ds(0, 2), slice(None), pl.ds(256, 128)),
            (pl.ds(3, 1), slice(None), pl.ds(0, 384)),
            (pl.ds(0, 4), slice(None), pl.ds(384, 128)),
        ][n]
        return pltpu.make_async_remote_copy(
            src_ref=rp.at[sl], dst_ref=rv.at[sl],
            send_sem=ret_send.at[n], recv_sem=ret_recv.at[n], device_id=nxt, device_id_type=MESH)

    def give_back(rows, quarters):
        parts = [[blk[jnp.where(c == 3, UP4, UP3), c, ri] for c in quarters] for ri in range(2)]
        re, im = [p[0] if len(p) == 1 else jnp.concatenate(p, axis=1) for p in parts]
        scale = 1.0 / math.sqrt(K)
        for ri, product in enumerate(products(1, rows, re, im)):
            scaled = (product * scale).astype(BF16)
            for i, c in enumerate(quarters):
                rp[c, ri, rows, :] = scaled[:, i * Q:(i + 1) * Q]

    def take_back(n):
        r, c = tile_at(n)
        rows, cols = pl.ds(pl.multiple_of(r * Q, Q), Q), pl.ds(pl.multiple_of(c * Q, Q), Q)
        slot = jnp.where(c == 3, 3, 2)
        flag = active[0, slot].astype(F32)
        ost[slot, :, rows, cols] = (rv[c, :, rows, :].astype(F32) * flag).astype(BF16)
        put_out(slot, rows, cols)

    def when_in(k, table):
        def run(body):
            entries = {key: v if isinstance(v, tuple) else (v,) for key, v in table.items()}
            first = pick(k, {key: v[0] for key, v in entries.items()})

            @pl.when(first >= 0)
            def _():
                rest = [pick(k, {key: v[i] for key, v in entries.items()}, 0)
                        for i in range(1, len(next(iter(entries.values()))))]
                body(first, *rest)
        return run

    flags.wait()
    first_transform()
    pl.semaphore_wait(barrier, WIN - 1 + 6)
    for part in range(4):
        spread(0, part)
    acc[...] = jnp.zeros_like(acc)

    @pl.loop(0, LAST_STEP - FIRST_STEP + 1)
    def _(step):
        k = step + FIRST_STEP

        @pl.when((k >= 0) & (k < PIECES))
        def _():
            wait_bytes(piece(UP4, k), z_recv.at[k])

            @pl.when((x <= 2) & (k < 24))
            def _():
                send_p(UP4, k)

            @pl.when(x == 0)
            def _():
                send_m(UP4, k)

        @pl.when((k >= -4) & (k < 0))
        def _():
            wait_bytes(wh.at[0, pl.ds(0, WIN - 1), 0, 0], aa_recv.at[FIRST + 4 + k])

        @when_in(k, GATHERED)
        def _(sc):
            wait_bytes(wh.at[sc, pl.ds(0, WIN - 1)], aa_recv.at[sc])

        lo = jnp.where(k < 0, k + 4, k + AHEAD + jnp.where(k > MORE_AHEAD, 1, 0))
        count = jnp.where((k >= -4) & (k != 0) & (lo < PIECES), jnp.where(k == MORE_AHEAD, 2, 1), 0)
        hi = lo + count

        @pl.loop(lo, hi)
        def _(j):
            send_z(j)

            @pl.when(x >= 1)
            def _():
                send_m(OWN, j)

            @pl.when((x == 3) & (j < 24))
            def _():
                send_p(OWN, j)

        @when_in(k, FORWARD)
        def _(first, last):
            @pl.loop(first, last)
            def _(w):
                rows = pl.ds(pl.multiple_of(w * 256, 256), 256)
                wait_bytes(blk.at[UP1, 3, :, rows, :], m_recv.at[12 + w])
                pltpu.make_async_remote_copy(
                    src_ref=blk.at[UP1, 3, :, rows, :], dst_ref=blk.at[UP3, 3, :, rows, :],
                    send_sem=a2_send, recv_sem=a2_recv.at[w], device_id=prv, device_id_type=MESH).start()

        @when_in(k, TRANSFORM)
        def _(sc):
            transform(sc)

        @when_in(k, SPREAD)
        def _(sc):
            spread(sc)

        @when_in(k, WAIT_M)
        def _(first, last):
            @pl.loop(first * 4, last * 4)
            def _(i):
                rows = pl.ds(pl.multiple_of(i % 4 * 256, 256), 256)
                wait_bytes(blk.at[UP1, i // 4, :, rows, :], m_recv.at[i])

        @when_in(k, WAIT_P)
        def _(first, last):
            @pl.loop(first, last)
            def _(quarter):
                wait_bytes(blk.at[UP3, quarter], p_recv.at[quarter])

        @when_in(k, TURN)
        def _(left, first, last):
            @pl.loop(first, last)
            def _(quarter):
                turn(left, quarter)

        @when_in(k, BACK_HALF)
        def _(_):
            give_back(pl.ds(0, 256), (0, 1))

        @when_in(k, BACK_TALL)
        def _(quarter):
            give_back(pl.ds(0, 384), (quarter,))

        @when_in(k, BACK_WIDE)
        def _(quarter, pair):
            give_back(pl.ds(pl.multiple_of(quarter * Q, Q), Q), (pair * 2, pair * 2 + 1))

        for at_k, ns in RETURN.items():
            now = k == (at_k if ns != (0,) else jnp.where(x == 3, RETURN_EARLY, at_k))

            @pl.when(now)
            def _():
                for n in ns:
                    ret_copy(n).start()

        @when_in(k, SUMMARY)
        def _(slot, half, pair):
            block = pick(slot, {0: OWN, 1: UP1, 3: UP3, 4: UP4}, 0)
            summary(slot, block, half, pair)

        @when_in(k, PART)
        def _(w):
            add_windows(w)

        for at_k, ns in TAKE.items():
            @pl.when(k == at_k)
            def _():
                for n in ns:
                    ret_copy(n).wait_recv()

        tiles = {key: (TILES_OF[ns[0]][0], TILES_OF[ns[-1]][1]) for key, ns in TAKE.items()}

        @when_in(k, tiles)
        def _(first, last):
            @pl.loop(first, last)
            def _(n):
                take_back(n)

    for n in range(5):
        ret_copy(n).wait_send()
    wait_bytes(blk.at[UP3, 3], a2_send)
    wait_bytes(blk.at[OWN], z_send)
    wait_bytes(blk.at[OWN], m_send)
    wait_bytes(blk.at[OWN, pl.ds(0, 3)], p_send)
    for sc in range(8):
        wait_bytes(wh.at[sc, pl.ds(0, WIN - 1)], aa_send.at[sc])
    pltpu.make_async_copy(ost, out, out_sem).wait()


def shards(records, active):
    dma = pltpu.SemaphoreType.DMA
    out = pl.pallas_call(
        kernel,
        out_shape=jax.ShapeDtypeStruct((SLOTS, 2, ST, ST), BF16),
        in_specs=[
            pl.BlockSpec(memory_space=pltpu.HBM),
            pl.BlockSpec(memory_space=pltpu.HBM),
            pl.BlockSpec(memory_space=pltpu.HBM),
        ],
        out_specs=pl.BlockSpec(memory_space=pl.ANY),
        scratch_shapes=[
            pltpu.SMEM((1, SLOTS), jnp.int32),
            pltpu.VMEM((2 * BINS, HALF), BF16),
            pltpu.VMEM((SLOTS_IN, 2 * Q, SAMPLES), BF16),
            pltpu.VMEM((8, WIN, 2, 2, BAND_BINS, Q), BF16),
            pltpu.VMEM((4, 4, 2, K, Q), BF16),
            pltpu.VMEM((2, 2, ST, K), BF16),
            pltpu.VMEM((4, 2, ST, Q), BF16),
            pltpu.VMEM((4, 2, ST, Q), BF16),
            pltpu.VMEM((SLOTS, 2, ST, ST), BF16),
            pltpu.VMEM((2, ST, 2 * Q), F32),
            dma((4,)), dma((4,)), dma((4,)), dma((SLOTS_IN,)), dma((8,)), dma((FIRST + 4,)), dma, dma((PIECES,)), dma, dma((16,)), dma, dma((3,)),
            dma, dma((4,)), dma((5,)), dma((5,)), dma, dma,
        ],
        compiler_params=pltpu.CompilerParams(
            collective_id=0, has_side_effects=True, vmem_limit_bytes=42 * 2**20),
        cost_estimate=pl.CostEstimate(flops=20 * 2**30, bytes_accessed=25 * 2**20, transcendentals=0),
    )(pltpu.with_memory_space_constraint(active, pltpu.HBM), records, pltpu.with_memory_space_constraint(jnp.asarray(spectral_table()), pltpu.HBM))
    return out.reshape(1, SLOTS, 1, 2 * ST, ST)


def solution(mesh):
    return jax.shard_map(
        shards,
        mesh=mesh,
        in_specs=(P("win", "blk", None), P("blk", None)),
        out_specs=P("blk", None, "win", None, None),
        check_vma=False,
    )
```

```python
import functools
import math

import jax
import jax.numpy as jnp
import ml_dtypes
import numpy as np
from jax import lax
from jax.experimental import pallas as pl
from jax.experimental.pallas import tpu as pltpu
from jax.sharding import PartitionSpec as P

SAMPLES = 4096
BINS = 256
BIN0 = 16
SLOTS = 5
BAND_BINS = 32
EPSILON = 1e-06

WIN = 8
RING = 4
BLOCKS = 16
LOCAL_W = 4
ST = 512
Q = 128
K = 1024
PIECES = 32
SLOTS_IN = 4

MESH = pl.DeviceIdType.MESH
F32 = jnp.float32
BF16 = jnp.bfloat16

OWN, UP4, UP1, UP3 = 0, 1, 2, 3


def spectral_table():
    phase = (np.arange(BINS)[:, None] + BIN0) * np.arange(HALF)[None, :] % SAMPLES
    angles = phase.astype(np.float32) * np.float32(2.0 * math.pi / SAMPLES)
    angles = angles.astype(np.float64)
    return np.concatenate([np.cos(angles), -np.sin(angles)]).astype(np.float32).astype(ml_dtypes.bfloat16)


def pick(k, table, default=-1):
    value = jnp.int32(default)
    for at_k, entry in table.items():
        value = jnp.where(k == at_k, jnp.int32(entry), value)
    return value


FIRST_STEP, LAST_STEP = -5, 43
HALF = SAMPLES // 2
PART_COLS = HALF // 4
SINGLE = 4
AHEAD = 4
FIRST = 8
TRANSFORM = {-5: 1, -1: 2, 2: 3, 6: 4, 9: 5, 11: 6, 13: 7}
SPREAD = {-4: 1, -1: 2, 2: 3, 6: 4, 9: 5, 11: 6, 13: 7}
GATHERED = {1: 1, 5: 2, 9: 3, 13: 4, 15: 5, 17: 6, 19: 7}
WAIT_M = {20: (0, 2), 26: (2, 3)}
WAIT_P = {21: (0, 2), 26: (2, 3)}
TURN = {9: (0, 0, 2), 19: (0, 2, 4), 20: (1, 0, 2), 26: (1, 2, 3), 33: (1, 3, 4)}
BACK_HALF = {21: 0}
BACK_TALL = {27: 2, 31: 3}
BACK_WIDE = {26: (2, 0), 33: (3, 0), 34: (3, 1)}
RETURN = {24: (0,), 27: (1, 2), 31: (3,), 34: (4,)}
RETURN_EARLY = 21
SUMMARY = {10: (0, 0, 0), 16: (4, 0, 0), 22: (1, 0, 0), 23: (3, 0, 0), 24: (0, 0, 1), 25: (0, 1, 0), 28: (0, 1, 1),
           29: (4, 1, 0), 30: (3, 1, 0), 32: (1, 1, 0), 35: (4, 0, 1), 36: (4, 1, 1), 37: (1, 0, 1), 38: (1, 1, 1)}
PART = {39: 0, 40: 1, 41: 2, 42: 3}
FORWARD = {33: (0, 4)}
TAKE = {31: (0,), 39: (1, 2), 41: (3,), 43: (4,)}
TILE_AT = [(0, 0), (0, 1), (1, 0), (1, 1), (0, 2), (1, 2), (2, 2), (2, 0), (2, 1),
           (0, 3), (1, 3), (2, 3), (3, 0), (3, 1), (3, 2), (3, 3)]
TILES_OF = [(0, 4), (4, 7), (7, 9), (9, 12), (12, 16)]


def kernel(active_in, rec, table, out, active, tab, rbuf, wh, blk, lt, rp, rv, ost, acc,
           tab_sem, first_sem, later_sem, rec_sem, aa_send, aa_recv, z_send, z_recv, m_send, m_recv, p_send, p_recv,
           a2_send, a2_recv, ret_send, ret_recv, out_sem, active_sem):
    me = lax.axis_index("win")
    b = lax.axis_index("blk")
    z, x = b // RING, b % RING

    def peer(i):
        return (lax.rem(me + i, WIN), b)

    def at(dz, dx):
        return (me, lax.rem(z + dz + RING, RING) * RING + lax.rem(x + dx + RING, RING))

    nxt = (me, lax.rem(b + 1, BLOCKS))
    prv = (me, lax.rem(b + BLOCKS - 1, BLOCKS))

    def load(sc):
        slot = sc % SLOTS_IN
        return pltpu.make_async_copy(
            rec.at[sc % LOCAL_W, pl.ds(pl.multiple_of(sc // LOCAL_W * 2 * Q, 2 * Q), 2 * Q), :],
            rbuf.at[slot], rec_sem.at[slot])

    def fetch(part):
        cols = pl.ds(pl.multiple_of(part * PART_COLS, PART_COLS), PART_COLS)
        later = pl.ds(pl.multiple_of(HALF + part * PART_COLS, PART_COLS), PART_COLS)
        return (pltpu.make_async_copy(table.at[:, cols], tab.at[:, cols], tab_sem.at[part]),
                pltpu.make_async_copy(rec.at[0, pl.ds(0, 2 * Q), cols], rbuf.at[0, :, cols], first_sem.at[part]),
                pltpu.make_async_copy(rec.at[0, pl.ds(0, 2 * Q), later], rbuf.at[0, :, later], later_sem.at[part]))

    for part in range(4):
        for copy in fetch(part):
            copy.start()
    flags = pltpu.make_async_copy(active_in, active, active_sem)
    flags.start()

    barrier = pltpu.get_barrier_semaphore()
    for i in range(1, WIN):
        pl.semaphore_signal(barrier, inc=1, device_id=peer(i), device_id_type=MESH)
    for dev in (at(-1, 0), at(1, 0), at(0, -1), at(0, 1), nxt, prv):
        pl.semaphore_signal(barrier, inc=1, device_id=dev, device_id_type=MESH)

    def against(table_rows, rows):
        return lax.dot_general(table_rows, rows, (((1,), (1,)), ((), ())), preferred_element_type=F32)

    def transform(sc):
        load(sc).wait()
        slot = sc % SLOTS_IN
        whiten(sc, against(tab[...], rbuf[slot, :, pl.ds(0, HALF)]), against(tab[...], rbuf[slot, :, pl.ds(HALF, HALF)]))

    def first_transform():
        acc[...] = jnp.zeros_like(acc)

        @pl.loop(0, 4)
        def _(part):
            for copy in fetch(part):
                copy.wait()
            cols = pl.ds(pl.multiple_of(part * PART_COLS, PART_COLS), PART_COLS)
            later = pl.ds(pl.multiple_of(HALF + part * PART_COLS, PART_COLS), PART_COLS)
            acc[0] += against(tab[:, cols], rbuf[0, :, cols])
            acc[1] += against(tab[:, cols], rbuf[0, :, later])

        for sc in range(1, SLOTS_IN):
            load(sc).start()
        whiten(0, acc[0], acc[1])

    def whiten(sc, early, later):
        odd = lax.broadcasted_iota(jnp.int32, early.shape, 0) % 2 == 1
        spectra = early + jnp.where(odd, -later, later)
        power = jnp.sum(spectra * spectra, axis=0, keepdims=True) / BINS
        white = (spectra * lax.rsqrt(power + EPSILON)).astype(BF16)
        for q in range(WIN):
            for ri in range(2):
                for qt in range(2):
                    wh[sc, q, qt, ri] = white[ri * BINS + q * BAND_BINS:ri * BINS + (q + 1) * BAND_BINS,
                                              qt * Q:(qt + 1) * Q]

        if isinstance(sc, int):
            load(sc + SLOTS_IN).start()
        else:
            @pl.when(sc + SLOTS_IN < 8)
            def _():
                load(sc + SLOTS_IN).start()

    def spread(sc, part=None):
        h, w = sc // LOCAL_W, sc % LOCAL_W
        row = pl.multiple_of((w * WIN + me) * BAND_BINS, BAND_BINS)

        @pl.loop(1, WIN)
        def _(i):
            to = peer(i)
            if part is None:
                src = wh.at[sc, to[0]]
                dst = blk.at[OWN, pl.ds(h * 2, 2), :, pl.ds(row, BAND_BINS), :]
            else:
                src = wh.at[sc, to[0], part // 2, part % 2]
                dst = blk.at[OWN, part // 2, part % 2, pl.ds(row, BAND_BINS), :]
            pltpu.make_async_remote_copy(
                src_ref=src, dst_ref=dst, send_sem=aa_send.at[sc],
                recv_sem=aa_recv.at[sc if part is None else FIRST + part],
                device_id=to, device_id_type=MESH,
            ).start()

        for own in range(4) if part is None else (part,):
            blk[OWN, h * 2 + own // 2, own % 2, pl.ds(row, BAND_BINS), :] = wh[sc, me, own // 2, own % 2]

    def place(j):
        early = j < 16
        return jnp.where(early, j // 2 % 2, j // 8), jnp.where(early, j // 4, j // 2 % 4)

    def piece(block, j, two):
        quarter, w = place(j)
        return blk.at[block, quarter, slice(None) if two else j % 2, pl.ds(pl.multiple_of(w * 256, 256), 256), :]

    def z_sem(j, two):
        return z_recv.at[SINGLE // 2 + j // 2 if two else j]

    def wait_bytes(ref, sem):
        pltpu.make_async_copy(ref, ref, sem).wait()

    def send_z(j, two):
        pltpu.make_async_remote_copy(
            src_ref=piece(OWN, j, two), dst_ref=piece(UP4, j, two),
            send_sem=z_send, recv_sem=z_sem(j, two), device_id=at(-1, 0), device_id_type=MESH).start()

    def send_m(block, j, two):
        quarter, w = place(j)
        pltpu.make_async_remote_copy(
            src_ref=piece(block, j, two), dst_ref=piece(UP1, j, two),
            send_sem=m_send, recv_sem=m_recv.at[quarter * 4 + w], device_id=at(0, -1), device_id_type=MESH).start()

    def send_p(block, j, two):
        quarter, _ = place(j)
        pltpu.make_async_remote_copy(
            src_ref=piece(block, j, two), dst_ref=piece(UP3, j, two),
            send_sem=p_send, recv_sem=p_recv.at[quarter], device_id=at(0, 1), device_id_type=MESH).start()

    def send_on(j, two):
        wait_bytes(piece(UP4, j, two), z_sem(j, two))

        @pl.when((x <= 2) & (j < 24))
        def _():
            send_p(UP4, j, two)

        @pl.when(x == 0)
        def _():
            send_m(UP4, j, two)

    def send_own(j, two):
        send_z(j, two)

        @pl.when(x >= 1)
        def _():
            send_m(OWN, j, two)

        @pl.when((x == 3) & (j < 24))
        def _():
            send_p(OWN, j, two)

    def turn(left, quarter):
        block = jnp.where(left == 0, OWN, UP1)
        for ri in range(2):
            lt[left, ri, pl.ds(pl.multiple_of(quarter * Q, Q), Q), :] = blk[block, quarter, ri].T

    def products(left, rows, re, im, window=slice(None)):
        lre, lim = lt[left, 0, rows, window], lt[left, 1, rows, window]
        dot = functools.partial(jnp.dot, preferred_element_type=F32)
        real = dot(lre, re) + dot(lim, im)
        imag = dot(lim, re) - dot(lre, im)
        return real, imag

    def put_out(slot, rows, cols):
        pltpu.make_async_copy(ost.at[slot, :, rows, cols], out.at[slot, :, rows, cols], out_sem).start()

    def summary(slot, block, half, pair):
        rows = pl.ds(pl.multiple_of(half * 256, 256), 256)
        cols = pl.ds(pl.multiple_of(pair * 256, 256), 256)
        scale = active[0, slot].astype(F32) * (1.0 / math.sqrt(K))
        re, im = [jnp.concatenate([blk[block, pair * 2 + i, ri] for i in range(2)], axis=1) for ri in range(2)]
        real, imag = products(0, rows, re, im)
        ost[slot, 0, rows, cols] = (real * scale).astype(BF16)
        ost[slot, 1, rows, cols] = (imag * scale).astype(BF16)
        put_out(slot, rows, cols)

    def add_windows(w):
        window = pl.ds(pl.multiple_of(w * 256, 256), 256)
        wait_bytes(blk.at[UP3, 3, :, window, :], a2_recv.at[w])

        @pl.loop(0, 2)
        def _(half):
            rows = pl.ds(pl.multiple_of(half * 256, 256), 256)
            re, im = [jnp.concatenate([blk[UP3, c, ri, window, :] for c in (2, 3)], axis=1) for ri in range(2)]
            real, imag = products(0, rows, re, im, window)
            acc[0, rows, :] += real
            acc[1, rows, :] += imag

            @pl.when(w == 3)
            def _():
                for slot, c in ((3, 2), (2, 3)):
                    scale = active[0, slot].astype(F32) * (1.0 / math.sqrt(K))
                    cols = pl.ds(c * Q, Q)
                    ost[slot, :, rows, cols] = (acc[:, rows, (c - 2) * Q:(c - 1) * Q] * scale).astype(BF16)
                    put_out(slot, rows, cols)

    def tile_at(n):
        return (pick(n, {i: rc[0] for i, rc in enumerate(TILE_AT)}, 0),
                pick(n, {i: rc[1] for i, rc in enumerate(TILE_AT)}, 0))

    def ret_copy(n):
        sl = [
            (pl.ds(0, 2), slice(None), pl.ds(0, 256)),
            (pl.ds(2, 1), slice(None), pl.ds(0, 384)),
            (pl.ds(0, 2), slice(None), pl.ds(256, 128)),
            (pl.ds(3, 1), slice(None), pl.ds(0, 384)),
            (pl.ds(0, 4), slice(None), pl.ds(384, 128)),
        ][n]
        return pltpu.make_async_remote_copy(
            src_ref=rp.at[sl], dst_ref=rv.at[sl],
            send_sem=ret_send.at[n], recv_sem=ret_recv.at[n], device_id=nxt, device_id_type=MESH)

    def give_back(rows, quarters):
        parts = [[blk[jnp.where(c == 3, UP4, UP3), c, ri] for c in quarters] for ri in range(2)]
        re, im = [p[0] if len(p) == 1 else jnp.concatenate(p, axis=1) for p in parts]
        scale = 1.0 / math.sqrt(K)
        for ri, product in enumerate(products(1, rows, re, im)):
            scaled = (product * scale).astype(BF16)
            for i, c in enumerate(quarters):
                rp[c, ri, rows, :] = scaled[:, i * Q:(i + 1) * Q]

    def take_back(n):
        r, c = tile_at(n)
        rows, cols = pl.ds(pl.multiple_of(r * Q, Q), Q), pl.ds(pl.multiple_of(c * Q, Q), Q)
        slot = jnp.where(c == 3, 3, 2)
        flag = active[0, slot].astype(F32)
        ost[slot, :, rows, cols] = (rv[c, :, rows, :].astype(F32) * flag).astype(BF16)
        put_out(slot, rows, cols)

    def when_in(k, table):
        def run(body):
            entries = {key: v if isinstance(v, tuple) else (v,) for key, v in table.items()}
            first = pick(k, {key: v[0] for key, v in entries.items()})

            @pl.when(first >= 0)
            def _():
                rest = [pick(k, {key: v[i] for key, v in entries.items()}, 0)
                        for i in range(1, len(next(iter(entries.values()))))]
                body(first, *rest)
        return run

    flags.wait()
    first_transform()
    pl.semaphore_wait(barrier, WIN - 1 + 6)
    for part in range(4):
        spread(0, part)
    acc[...] = jnp.zeros_like(acc)

    @pl.loop(0, LAST_STEP - FIRST_STEP + 1)
    def _(step):
        k = step + FIRST_STEP

        @pl.when((k >= 0) & (k < SINGLE))
        def _():
            send_on(k, False)

        @pl.when((k >= SINGLE) & (k < PIECES) & (k % 2 == 1))
        def _():
            send_on(k, True)

        @pl.when((k >= -SINGLE) & (k < 0))
        def _():
            wait_bytes(wh.at[0, pl.ds(0, WIN - 1), 0, 0], aa_recv.at[FIRST + 4 + k])
            send_own(k + SINGLE, False)

        @when_in(k, GATHERED)
        def _(sc):
            wait_bytes(wh.at[sc, pl.ds(0, WIN - 1)], aa_recv.at[sc])

        @pl.when((k >= 0) & (k + AHEAD < PIECES) & (k % 2 == 1))
        def _():
            send_own(k + AHEAD, True)

        @when_in(k, FORWARD)
        def _(first, last):
            @pl.loop(first, last)
            def _(w):
                rows = pl.ds(pl.multiple_of(w * 256, 256), 256)
                wait_bytes(blk.at[UP1, 3, :, rows, :], m_recv.at[12 + w])
                pltpu.make_async_remote_copy(
                    src_ref=blk.at[UP1, 3, :, rows, :], dst_ref=blk.at[UP3, 3, :, rows, :],
                    send_sem=a2_send, recv_sem=a2_recv.at[w], device_id=prv, device_id_type=MESH).start()

        @when_in(k, TRANSFORM)
        def _(sc):
            transform(sc)

        @when_in(k, SPREAD)
        def _(sc):
            spread(sc)

        @when_in(k, WAIT_M)
        def _(first, last):
            @pl.loop(first * 4, last * 4)
            def _(i):
                rows = pl.ds(pl.multiple_of(i % 4 * 256, 256), 256)
                wait_bytes(blk.at[UP1, i // 4, :, rows, :], m_recv.at[i])

        @when_in(k, WAIT_P)
        def _(first, last):
            @pl.loop(first, last)
            def _(quarter):
                wait_bytes(blk.at[UP3, quarter], p_recv.at[quarter])

        @when_in(k, TURN)
        def _(left, first, last):
            @pl.loop(first, last)
            def _(quarter):
                turn(left, quarter)

        @when_in(k, BACK_HALF)
        def _(_):
            give_back(pl.ds(0, 256), (0, 1))

        @when_in(k, BACK_TALL)
        def _(quarter):
            give_back(pl.ds(0, 384), (quarter,))

        @when_in(k, BACK_WIDE)
        def _(quarter, pair):
            give_back(pl.ds(pl.multiple_of(quarter * Q, Q), Q), (pair * 2, pair * 2 + 1))

        for at_k, ns in RETURN.items():
            now = k == (at_k if ns != (0,) else jnp.where(x == 3, RETURN_EARLY, at_k))

            @pl.when(now)
            def _():
                for n in ns:
                    ret_copy(n).start()

        @when_in(k, SUMMARY)
        def _(slot, half, pair):
            block = pick(slot, {0: OWN, 1: UP1, 3: UP3, 4: UP4}, 0)
            summary(slot, block, half, pair)

        @when_in(k, PART)
        def _(w):
            add_windows(w)

        for at_k, ns in TAKE.items():
            @pl.when(k == at_k)
            def _():
                for n in ns:
                    ret_copy(n).wait_recv()

        tiles = {key: (TILES_OF[ns[0]][0], TILES_OF[ns[-1]][1]) for key, ns in TAKE.items()}

        @when_in(k, tiles)
        def _(first, last):
            @pl.loop(first, last)
            def _(n):
                take_back(n)

    for n in range(5):
        ret_copy(n).wait_send()
    wait_bytes(blk.at[UP3, 3], a2_send)
    wait_bytes(blk.at[OWN], z_send)
    wait_bytes(blk.at[OWN], m_send)
    wait_bytes(blk.at[OWN, pl.ds(0, 3)], p_send)
    for sc in range(8):
        wait_bytes(wh.at[sc, pl.ds(0, WIN - 1)], aa_send.at[sc])
    pltpu.make_async_copy(ost, out, out_sem).wait()


def shards(records, active):
    dma = pltpu.SemaphoreType.DMA
    out = pl.pallas_call(
        kernel,
        out_shape=jax.ShapeDtypeStruct((SLOTS, 2, ST, ST), BF16),
        in_specs=[
            pl.BlockSpec(memory_space=pltpu.HBM),
            pl.BlockSpec(memory_space=pltpu.HBM),
            pl.BlockSpec(memory_space=pltpu.HBM),
        ],
        out_specs=pl.BlockSpec(memory_space=pl.ANY),
        scratch_shapes=[
            pltpu.SMEM((1, SLOTS), jnp.int32),
            pltpu.VMEM((2 * BINS, HALF), BF16),
            pltpu.VMEM((SLOTS_IN, 2 * Q, SAMPLES), BF16),
            pltpu.VMEM((8, WIN, 2, 2, BAND_BINS, Q), BF16),
            pltpu.VMEM((4, 4, 2, K, Q), BF16),
            pltpu.VMEM((2, 2, ST, K), BF16),
            pltpu.VMEM((4, 2, ST, Q), BF16),
            pltpu.VMEM((4, 2, ST, Q), BF16),
            pltpu.VMEM((SLOTS, 2, ST, ST), BF16),
            pltpu.VMEM((2, ST, 2 * Q), F32),
            dma((4,)), dma((4,)), dma((4,)), dma((SLOTS_IN,)), dma((8,)), dma((FIRST + 4,)), dma, dma(((SINGLE + PIECES) // 2,)), dma, dma((16,)), dma, dma((3,)),
            dma, dma((4,)), dma((5,)), dma((5,)), dma, dma,
        ],
        compiler_params=pltpu.CompilerParams(
            collective_id=0, has_side_effects=True, vmem_limit_bytes=42 * 2**20),
        cost_estimate=pl.CostEstimate(flops=20 * 2**30, bytes_accessed=25 * 2**20, transcendentals=0),
    )(pltpu.with_memory_space_constraint(active, pltpu.HBM), records, pltpu.with_memory_space_constraint(jnp.asarray(spectral_table()), pltpu.HBM))
    return out.reshape(1, SLOTS, 1, 2 * ST, ST)


def solution(mesh):
    return jax.shard_map(
        shards,
        mesh=mesh,
        in_specs=(P("win", "blk", None), P("blk", None)),
        out_specs=P("blk", None, "win", None, None),
        check_vma=False,
    )
```

```python
import functools
import math

import jax
import jax.numpy as jnp
import ml_dtypes
import numpy as np
from jax import lax
from jax.experimental import pallas as pl
from jax.experimental.pallas import tpu as pltpu
from jax.sharding import PartitionSpec as P

SAMPLES = 4096
BINS = 256
BIN0 = 16
SLOTS = 5
BAND_BINS = 32
EPSILON = 1e-06

WIN = 8
RING = 4
BLOCKS = 16
LOCAL_W = 4
ST = 512
Q = 128
K = 1024
PIECES = 32
SLOTS_IN = 4

MESH = pl.DeviceIdType.MESH
F32 = jnp.float32
BF16 = jnp.bfloat16

OWN, UP4, UP1, UP3 = 0, 1, 2, 3


def spectral_table():
    phase = (np.arange(BINS)[:, None] + BIN0) * np.arange(HALF)[None, :] % SAMPLES
    angles = phase.astype(np.float32) * np.float32(2.0 * math.pi / SAMPLES)
    angles = angles.astype(np.float64)
    return np.concatenate([np.cos(angles), -np.sin(angles)]).astype(np.float32).astype(ml_dtypes.bfloat16)


def pick(k, table, default=-1):
    value = jnp.int32(default)
    for at_k, entry in table.items():
        value = jnp.where(k == at_k, jnp.int32(entry), value)
    return value


FIRST_STEP, LAST_STEP = -5, 43
HALF = SAMPLES // 2
PARTS = 2
PART_COLS = HALF // PARTS
SINGLE = 4
AHEAD = 4
FIRST = 8
TRANSFORM = {-5: 1, -1: 2, 2: 3, 6: 4, 9: 5, 11: 6, 13: 7}
SPREAD = {-4: 1, -1: 2, 2: 3, 6: 4, 9: 5, 11: 6, 13: 7}
GATHERED = {1: 1, 5: 2, 9: 3, 13: 4, 15: 5, 17: 6, 19: 7}
WAIT_M = {20: (0, 2), 26: (2, 3)}
WAIT_P = {21: (0, 2), 26: (2, 3)}
TURN = {9: (0, 0, 2), 19: (0, 2, 4), 20: (1, 0, 2), 26: (1, 2, 3), 33: (1, 3, 4)}
BACK_HALF = {21: 0}
BACK_TALL = {27: 2, 31: 3}
BACK_WIDE = {26: (2, 0), 33: (3, 0), 34: (3, 1)}
RETURN = {24: (0,), 27: (1, 2), 31: (3,), 33: (4,), 34: (5,)}
RETURN_EARLY = 21
SUMMARY = {10: (0, 0, 0), 16: (4, 0, 0), 22: (1, 0, 0), 23: (3, 0, 0), 24: (0, 0, 1), 25: (0, 1, 0), 28: (0, 1, 1),
           29: (4, 1, 0), 30: (3, 1, 0), 32: (1, 1, 0), 35: (4, 0, 1), 36: (4, 1, 1), 37: (1, 0, 1), 38: (1, 1, 1)}
PART = {39: 0, 40: 1, 41: 2, 42: 3}
FORWARD = {33: (0, 4)}
TAKE = {31: (0,), 39: (1, 2), 41: (3,), 43: (4, 5)}
TILE_AT = [(0, 0), (0, 1), (1, 0), (1, 1), (0, 2), (1, 2), (2, 2), (2, 0), (2, 1),
           (0, 3), (1, 3), (2, 3), (3, 0), (3, 1), (3, 2), (3, 3)]
TILES_OF = [(0, 4), (4, 7), (7, 9), (9, 12), (12, 14), (14, 16)]


def kernel(active_in, rec, table, out, active, tab, rbuf, wh, blk, lt, rp, rv, ost, acc,
           tab_sem, first_sem, later_sem, rec_sem, aa_send, aa_recv, z_send, z_recv, m_send, m_recv, p_send, p_recv,
           a2_send, a2_recv, ret_send, ret_recv, out_sem, active_sem):
    me = lax.axis_index("win")
    b = lax.axis_index("blk")
    z, x = b // RING, b % RING

    def peer(i):
        return (lax.rem(me + i, WIN), b)

    def at(dz, dx):
        return (me, lax.rem(z + dz + RING, RING) * RING + lax.rem(x + dx + RING, RING))

    nxt = (me, lax.rem(b + 1, BLOCKS))
    prv = (me, lax.rem(b + BLOCKS - 1, BLOCKS))

    def load(sc):
        slot = sc % SLOTS_IN
        return pltpu.make_async_copy(
            rec.at[sc % LOCAL_W, pl.ds(pl.multiple_of(sc // LOCAL_W * 2 * Q, 2 * Q), 2 * Q), :],
            rbuf.at[slot], rec_sem.at[slot])

    def fetch(part):
        cols = pl.ds(pl.multiple_of(part * PART_COLS, PART_COLS), PART_COLS)
        later = pl.ds(pl.multiple_of(HALF + part * PART_COLS, PART_COLS), PART_COLS)
        return (pltpu.make_async_copy(table.at[:, cols], tab.at[:, cols], tab_sem.at[part]),
                pltpu.make_async_copy(rec.at[0, pl.ds(0, 2 * Q), cols], rbuf.at[0, :, cols], first_sem.at[part]),
                pltpu.make_async_copy(rec.at[0, pl.ds(0, 2 * Q), later], rbuf.at[0, :, later], later_sem.at[part]))

    for part in range(PARTS):
        for copy in fetch(part):
            copy.start()
    flags = pltpu.make_async_copy(active_in, active, active_sem)
    flags.start()

    barrier = pltpu.get_barrier_semaphore()
    for i in range(1, WIN):
        pl.semaphore_signal(barrier, inc=1, device_id=peer(i), device_id_type=MESH)
    for dev in (at(-1, 0), at(1, 0), at(0, -1), at(0, 1), nxt, prv):
        pl.semaphore_signal(barrier, inc=1, device_id=dev, device_id_type=MESH)

    def against(table_rows, rows):
        return lax.dot_general(table_rows, rows, (((1,), (1,)), ((), ())), preferred_element_type=F32)

    def transform(sc):
        load(sc).wait()
        slot = sc % SLOTS_IN
        whiten(sc, against(tab[...], rbuf[slot, :, pl.ds(0, HALF)]), against(tab[...], rbuf[slot, :, pl.ds(HALF, HALF)]))

    def first_transform():
        acc[...] = jnp.zeros_like(acc)

        @pl.loop(0, PARTS)
        def _(part):
            for copy in fetch(part):
                copy.wait()
            cols = pl.ds(pl.multiple_of(part * PART_COLS, PART_COLS), PART_COLS)
            later = pl.ds(pl.multiple_of(HALF + part * PART_COLS, PART_COLS), PART_COLS)
            acc[0] += against(tab[:, cols], rbuf[0, :, cols])
            acc[1] += against(tab[:, cols], rbuf[0, :, later])

        for sc in range(1, SLOTS_IN):
            load(sc).start()
        whiten(0, acc[0], acc[1])

    def whiten(sc, early, later):
        odd = lax.broadcasted_iota(jnp.int32, early.shape, 0) % 2 == 1
        spectra = early + jnp.where(odd, -later, later)
        power = jnp.sum(spectra * spectra, axis=0, keepdims=True) / BINS
        white = (spectra * lax.rsqrt(power + EPSILON)).astype(BF16)
        for q in range(WIN):
            for ri in range(2):
                for qt in range(2):
                    wh[sc, q, qt, ri] = white[ri * BINS + q * BAND_BINS:ri * BINS + (q + 1) * BAND_BINS,
                                              qt * Q:(qt + 1) * Q]

        if isinstance(sc, int):
            load(sc + SLOTS_IN).start()
        else:
            @pl.when(sc + SLOTS_IN < 8)
            def _():
                load(sc + SLOTS_IN).start()

    def spread(sc, part=None):
        h, w = sc // LOCAL_W, sc % LOCAL_W
        row = pl.multiple_of((w * WIN + me) * BAND_BINS, BAND_BINS)

        @pl.loop(1, WIN)
        def _(i):
            to = peer(i)
            if part is None:
                src = wh.at[sc, to[0]]
                dst = blk.at[OWN, pl.ds(h * 2, 2), :, pl.ds(row, BAND_BINS), :]
            else:
                src = wh.at[sc, to[0], part // 2, part % 2]
                dst = blk.at[OWN, part // 2, part % 2, pl.ds(row, BAND_BINS), :]
            pltpu.make_async_remote_copy(
                src_ref=src, dst_ref=dst, send_sem=aa_send.at[sc],
                recv_sem=aa_recv.at[sc if part is None else FIRST + part],
                device_id=to, device_id_type=MESH,
            ).start()

        for own in range(4) if part is None else (part,):
            blk[OWN, h * 2 + own // 2, own % 2, pl.ds(row, BAND_BINS), :] = wh[sc, me, own // 2, own % 2]

    def place(j):
        early = j < 16
        return jnp.where(early, j // 2 % 2, j // 8), jnp.where(early, j // 4, j // 2 % 4)

    def piece(block, j, two):
        quarter, w = place(j)
        return blk.at[block, quarter, slice(None) if two else j % 2, pl.ds(pl.multiple_of(w * 256, 256), 256), :]

    def z_sem(j, two):
        return z_recv.at[SINGLE // 2 + j // 2 if two else j]

    def wait_bytes(ref, sem):
        pltpu.make_async_copy(ref, ref, sem).wait()

    def send_z(j, two):
        pltpu.make_async_remote_copy(
            src_ref=piece(OWN, j, two), dst_ref=piece(UP4, j, two),
            send_sem=z_send, recv_sem=z_sem(j, two), device_id=at(-1, 0), device_id_type=MESH).start()

    def send_m(block, j, two):
        quarter, w = place(j)
        pltpu.make_async_remote_copy(
            src_ref=piece(block, j, two), dst_ref=piece(UP1, j, two),
            send_sem=m_send, recv_sem=m_recv.at[quarter * 4 + w], device_id=at(0, -1), device_id_type=MESH).start()

    def send_p(block, j, two):
        quarter, _ = place(j)
        pltpu.make_async_remote_copy(
            src_ref=piece(block, j, two), dst_ref=piece(UP3, j, two),
            send_sem=p_send, recv_sem=p_recv.at[quarter], device_id=at(0, 1), device_id_type=MESH).start()

    def send_on(j, two):
        wait_bytes(piece(UP4, j, two), z_sem(j, two))

        @pl.when((x <= 2) & (j < 24))
        def _():
            send_p(UP4, j, two)

        @pl.when(x == 0)
        def _():
            send_m(UP4, j, two)

    def send_own(j, two):
        send_z(j, two)

        @pl.when(x >= 1)
        def _():
            send_m(OWN, j, two)

        @pl.when((x == 3) & (j < 24))
        def _():
            send_p(OWN, j, two)

    def turn(left, quarter):
        block = jnp.where(left == 0, OWN, UP1)
        for ri in range(2):
            lt[left, ri, pl.ds(pl.multiple_of(quarter * Q, Q), Q), :] = blk[block, quarter, ri].T

    def products(left, rows, re, im, window=slice(None)):
        lre, lim = lt[left, 0, rows, window], lt[left, 1, rows, window]
        dot = functools.partial(jnp.dot, preferred_element_type=F32)
        real = dot(lre, re) + dot(lim, im)
        imag = dot(lim, re) - dot(lre, im)
        return real, imag

    def put_out(slot, rows, cols):
        pltpu.make_async_copy(ost.at[slot, :, rows, cols], out.at[slot, :, rows, cols], out_sem).start()

    def summary(slot, block, half, pair):
        rows = pl.ds(pl.multiple_of(half * 256, 256), 256)
        cols = pl.ds(pl.multiple_of(pair * 256, 256), 256)
        scale = active[0, slot].astype(F32) * (1.0 / math.sqrt(K))
        re, im = [jnp.concatenate([blk[block, pair * 2 + i, ri] for i in range(2)], axis=1) for ri in range(2)]
        real, imag = products(0, rows, re, im)
        ost[slot, 0, rows, cols] = (real * scale).astype(BF16)
        ost[slot, 1, rows, cols] = (imag * scale).astype(BF16)
        put_out(slot, rows, cols)

    def add_windows(w):
        window = pl.ds(pl.multiple_of(w * 256, 256), 256)
        wait_bytes(blk.at[UP3, 3, :, window, :], a2_recv.at[w])

        @pl.loop(0, 2)
        def _(half):
            rows = pl.ds(pl.multiple_of(half * 256, 256), 256)
            re, im = [jnp.concatenate([blk[UP3, c, ri, window, :] for c in (2, 3)], axis=1) for ri in range(2)]
            real, imag = products(0, rows, re, im, window)
            acc[0, rows, :] += real
            acc[1, rows, :] += imag

            @pl.when(w == 3)
            def _():
                for slot, c in ((3, 2), (2, 3)):
                    scale = active[0, slot].astype(F32) * (1.0 / math.sqrt(K))
                    cols = pl.ds(c * Q, Q)
                    ost[slot, :, rows, cols] = (acc[:, rows, (c - 2) * Q:(c - 1) * Q] * scale).astype(BF16)
                    put_out(slot, rows, cols)

    def tile_at(n):
        return (pick(n, {i: rc[0] for i, rc in enumerate(TILE_AT)}, 0),
                pick(n, {i: rc[1] for i, rc in enumerate(TILE_AT)}, 0))

    def ret_copy(n):
        sl = [
            (pl.ds(0, 2), slice(None), pl.ds(0, 256)),
            (pl.ds(2, 1), slice(None), pl.ds(0, 384)),
            (pl.ds(0, 2), slice(None), pl.ds(256, 128)),
            (pl.ds(3, 1), slice(None), pl.ds(0, 384)),
            (pl.ds(0, 2), slice(None), pl.ds(384, 128)),
            (pl.ds(2, 2), slice(None), pl.ds(384, 128)),
        ][n]
        return pltpu.make_async_remote_copy(
            src_ref=rp.at[sl], dst_ref=rv.at[sl],
            send_sem=ret_send.at[n], recv_sem=ret_recv.at[n], device_id=nxt, device_id_type=MESH)

    def give_back(rows, quarters):
        parts = [[blk[jnp.where(c == 3, UP4, UP3), c, ri] for c in quarters] for ri in range(2)]
        re, im = [p[0] if len(p) == 1 else jnp.concatenate(p, axis=1) for p in parts]
        scale = 1.0 / math.sqrt(K)
        for ri, product in enumerate(products(1, rows, re, im)):
            scaled = (product * scale).astype(BF16)
            for i, c in enumerate(quarters):
                rp[c, ri, rows, :] = scaled[:, i * Q:(i + 1) * Q]

    def take_back(n):
        r, c = tile_at(n)
        rows, cols = pl.ds(pl.multiple_of(r * Q, Q), Q), pl.ds(pl.multiple_of(c * Q, Q), Q)
        slot = jnp.where(c == 3, 3, 2)
        flag = active[0, slot].astype(F32)
        ost[slot, :, rows, cols] = (rv[c, :, rows, :].astype(F32) * flag).astype(BF16)
        put_out(slot, rows, cols)

    def when_in(k, table):
        def run(body):
            entries = {key: v if isinstance(v, tuple) else (v,) for key, v in table.items()}
            first = pick(k, {key: v[0] for key, v in entries.items()})

            @pl.when(first >= 0)
            def _():
                rest = [pick(k, {key: v[i] for key, v in entries.items()}, 0)
                        for i in range(1, len(next(iter(entries.values()))))]
                body(first, *rest)
        return run

    flags.wait()
    first_transform()
    pl.semaphore_wait(barrier, WIN - 1 + 6)
    for part in range(4):
        spread(0, part)
    acc[...] = jnp.zeros_like(acc)

    @pl.loop(0, LAST_STEP - FIRST_STEP + 1)
    def _(step):
        k = step + FIRST_STEP

        @pl.when((k >= 0) & (k < SINGLE))
        def _():
            send_on(k, False)

        @pl.when((k >= SINGLE) & (k < PIECES) & (k % 2 == 1))
        def _():
            send_on(k, True)

        @pl.when((k >= -SINGLE) & (k < 0))
        def _():
            wait_bytes(wh.at[0, pl.ds(0, WIN - 1), 0, 0], aa_recv.at[FIRST + 4 + k])
            send_own(k + SINGLE, False)

        @when_in(k, GATHERED)
        def _(sc):
            wait_bytes(wh.at[sc, pl.ds(0, WIN - 1)], aa_recv.at[sc])

        @pl.when((k >= 0) & (k + AHEAD < PIECES) & (k % 2 == 1))
        def _():
            send_own(k + AHEAD, True)

        @when_in(k, FORWARD)
        def _(first, last):
            @pl.loop(first, last)
            def _(w):
                rows = pl.ds(pl.multiple_of(w * 256, 256), 256)
                wait_bytes(blk.at[UP1, 3, :, rows, :], m_recv.at[12 + w])
                pltpu.make_async_remote_copy(
                    src_ref=blk.at[UP1, 3, :, rows, :], dst_ref=blk.at[UP3, 3, :, rows, :],
                    send_sem=a2_send, recv_sem=a2_recv.at[w], device_id=prv, device_id_type=MESH).start()

        @when_in(k, TRANSFORM)
        def _(sc):
            transform(sc)

        @when_in(k, SPREAD)
        def _(sc):
            spread(sc)

        @when_in(k, WAIT_M)
        def _(first, last):
            @pl.loop(first * 4, last * 4)
            def _(i):
                rows = pl.ds(pl.multiple_of(i % 4 * 256, 256), 256)
                wait_bytes(blk.at[UP1, i // 4, :, rows, :], m_recv.at[i])

        @when_in(k, WAIT_P)
        def _(first, last):
            @pl.loop(first, last)
            def _(quarter):
                wait_bytes(blk.at[UP3, quarter], p_recv.at[quarter])

        @when_in(k, TURN)
        def _(left, first, last):
            @pl.loop(first, last)
            def _(quarter):
                turn(left, quarter)

        @when_in(k, BACK_HALF)
        def _(_):
            give_back(pl.ds(0, 256), (0, 1))

        @when_in(k, BACK_TALL)
        def _(quarter):
            give_back(pl.ds(0, 384), (quarter,))

        @when_in(k, BACK_WIDE)
        def _(quarter, pair):
            give_back(pl.ds(pl.multiple_of(quarter * Q, Q), Q), (pair * 2, pair * 2 + 1))

        for at_k, ns in RETURN.items():
            now = k == (at_k if ns != (0,) else jnp.where(x == 3, RETURN_EARLY, at_k))

            @pl.when(now)
            def _():
                for n in ns:
                    ret_copy(n).start()

        @when_in(k, SUMMARY)
        def _(slot, half, pair):
            block = pick(slot, {0: OWN, 1: UP1, 3: UP3, 4: UP4}, 0)
            summary(slot, block, half, pair)

        @when_in(k, PART)
        def _(w):
            add_windows(w)

        for at_k, ns in TAKE.items():
            @pl.when(k == at_k)
            def _():
                for n in ns:
                    ret_copy(n).wait_recv()

        tiles = {key: (TILES_OF[ns[0]][0], TILES_OF[ns[-1]][1]) for key, ns in TAKE.items()}

        @when_in(k, tiles)
        def _(first, last):
            @pl.loop(first, last)
            def _(n):
                take_back(n)

    for n in range(6):
        ret_copy(n).wait_send()
    wait_bytes(blk.at[UP3, 3], a2_send)
    wait_bytes(blk.at[OWN], z_send)
    wait_bytes(blk.at[OWN], m_send)
    wait_bytes(blk.at[OWN, pl.ds(0, 3)], p_send)
    for sc in range(8):
        wait_bytes(wh.at[sc, pl.ds(0, WIN - 1)], aa_send.at[sc])
    pltpu.make_async_copy(ost, out, out_sem).wait()


def shards(records, active):
    dma = pltpu.SemaphoreType.DMA
    out = pl.pallas_call(
        kernel,
        out_shape=jax.ShapeDtypeStruct((SLOTS, 2, ST, ST), BF16),
        in_specs=[
            pl.BlockSpec(memory_space=pltpu.HBM),
            pl.BlockSpec(memory_space=pltpu.HBM),
            pl.BlockSpec(memory_space=pltpu.HBM),
        ],
        out_specs=pl.BlockSpec(memory_space=pl.ANY),
        scratch_shapes=[
            pltpu.SMEM((1, SLOTS), jnp.int32),
            pltpu.VMEM((2 * BINS, HALF), BF16),
            pltpu.VMEM((SLOTS_IN, 2 * Q, SAMPLES), BF16),
            pltpu.VMEM((8, WIN, 2, 2, BAND_BINS, Q), BF16),
            pltpu.VMEM((4, 4, 2, K, Q), BF16),
            pltpu.VMEM((2, 2, ST, K), BF16),
            pltpu.VMEM((4, 2, ST, Q), BF16),
            pltpu.VMEM((4, 2, ST, Q), BF16),
            pltpu.VMEM((SLOTS, 2, ST, ST), BF16),
            pltpu.VMEM((2, ST, 2 * Q), F32),
            dma((PARTS,)), dma((PARTS,)), dma((PARTS,)), dma((SLOTS_IN,)), dma((8,)), dma((FIRST + 4,)), dma, dma(((SINGLE + PIECES) // 2,)), dma, dma((16,)), dma, dma((3,)),
            dma, dma((4,)), dma((6,)), dma((6,)), dma, dma,
        ],
        compiler_params=pltpu.CompilerParams(
            collective_id=0, has_side_effects=True, vmem_limit_bytes=42 * 2**20),
        cost_estimate=pl.CostEstimate(flops=20 * 2**30, bytes_accessed=25 * 2**20, transcendentals=0),
    )(pltpu.with_memory_space_constraint(active, pltpu.HBM), records, pltpu.with_memory_space_constraint(jnp.asarray(spectral_table()), pltpu.HBM))
    return out.reshape(1, SLOTS, 1, 2 * ST, ST)


def solution(mesh):
    return jax.shard_map(
        shards,
        mesh=mesh,
        in_specs=(P("win", "blk", None), P("blk", None)),
        out_specs=P("blk", None, "win", None, None),
        check_vma=False,
    )
```

```python
import functools
import math

import jax
import jax.numpy as jnp
import ml_dtypes
import numpy as np
from jax import lax
from jax.experimental import pallas as pl
from jax.experimental.pallas import tpu as pltpu
from jax.sharding import PartitionSpec as P

SAMPLES = 4096
BINS = 256
BIN0 = 16
SLOTS = 5
BAND_BINS = 32
EPSILON = 1e-06

WIN = 8
RING = 4
BLOCKS = 16
LOCAL_W = 4
ST = 512
Q = 128
K = 1024
PIECES = 32
SLOTS_IN = 4

MESH = pl.DeviceIdType.MESH
F32 = jnp.float32
BF16 = jnp.bfloat16

OWN, UP4, UP1, UP3 = 0, 1, 2, 3


def spectral_table():
    phase = (np.arange(BINS)[:, None] + BIN0) * np.arange(HALF)[None, :] % SAMPLES
    angles = phase.astype(np.float32) * np.float32(2.0 * math.pi / SAMPLES)
    angles = angles.astype(np.float64)
    return np.concatenate([np.cos(angles), -np.sin(angles)]).astype(np.float32).astype(ml_dtypes.bfloat16)


def pick(k, table, default=-1):
    value = jnp.int32(default)
    for at_k, entry in table.items():
        value = jnp.where(k == at_k, jnp.int32(entry), value)
    return value


FIRST_STEP, LAST_STEP = -5, 43
HALF = SAMPLES // 2
PARTS = 2
PART_COLS = HALF // PARTS
SINGLE = 4
AHEAD = 4
FIRST = 8
TRANSFORM = {-5: 1, -1: 2, 2: 3, 6: 4, 9: 5, 11: 6, 13: 7}
SPREAD = {-4: 1, -1: 2, 2: 3, 6: 4, 9: 5, 11: 6, 13: 7}
GATHERED = {1: 1, 5: 2, 9: 3, 13: 4, 15: 5, 17: 6, 19: 7}
WAIT_M = {20: (0, 2), 26: (2, 3)}
WAIT_P = {21: (0, 2), 26: (2, 3)}
TURN = {9: (0, 0, 2), 19: (0, 2, 4), 20: (1, 0, 2), 26: (1, 2, 3), 33: (1, 3, 4)}
BACK_HALF = {21: 0}
BACK_TALL = {27: 2, 31: 3}
BACK_WIDE = {26: (2, 0), 33: (3, 0), 34: (3, 1)}
RETURN = {24: (0,), 27: (1, 2), 31: (3,), 33: (4,), 34: (5,)}
RETURN_EARLY = 21
SUMMARY = {10: (0, 0, 0), 16: (4, 0, 0), 22: (1, 0, 0), 23: (3, 0, 0), 24: (0, 0, 1), 25: (0, 1, 0), 28: (0, 1, 1),
           29: (4, 1, 0), 30: (3, 1, 0), 32: (1, 1, 0), 35: (4, 0, 1), 36: (4, 1, 1), 37: (1, 0, 1), 38: (1, 1, 1)}
PART = {39: 0, 40: 1, 41: 2, 42: 3}
FORWARD = {33: (0, 4)}
TAKE = {31: (0,), 39: (1, 2), 41: (3,), 43: (4, 5)}
TILE_AT = [(0, 0), (0, 1), (1, 0), (1, 1), (0, 2), (1, 2), (2, 2), (2, 0), (2, 1),
           (0, 3), (1, 3), (2, 3), (3, 0), (3, 1), (3, 2), (3, 3)]
TILES_OF = [(0, 4), (4, 7), (7, 9), (9, 12), (12, 14), (14, 16)]


def kernel(active_in, rec, table, out, active, tab, rbuf, wh, blk, lt, rp, rv, ost, acc,
           tab_sem, first_sem, later_sem, rec_sem, aa_send, aa_recv, z_send, z_recv, m_send, m_recv, p_send, p_recv,
           a2_send, a2_recv, ret_send, ret_recv, out_sem, active_sem):
    me = lax.axis_index("win")
    b = lax.axis_index("blk")
    z, x = b // RING, b % RING

    def peer(i):
        return (lax.rem(me + i, WIN), b)

    def at(dz, dx):
        return (me, lax.rem(z + dz + RING, RING) * RING + lax.rem(x + dx + RING, RING))

    nxt = (me, lax.rem(b + 1, BLOCKS))
    prv = (me, lax.rem(b + BLOCKS - 1, BLOCKS))

    def load(sc):
        slot = sc % SLOTS_IN
        return pltpu.make_async_copy(
            rec.at[sc % LOCAL_W, pl.ds(pl.multiple_of(sc // LOCAL_W * 2 * Q, 2 * Q), 2 * Q), :],
            rbuf.at[slot], rec_sem.at[slot])

    def fetch(part):
        cols = pl.ds(pl.multiple_of(part * PART_COLS, PART_COLS), PART_COLS)
        later = pl.ds(pl.multiple_of(HALF + part * PART_COLS, PART_COLS), PART_COLS)
        return (pltpu.make_async_copy(table.at[:, cols], tab.at[:, cols], tab_sem.at[part]),
                pltpu.make_async_copy(rec.at[0, pl.ds(0, 2 * Q), cols], rbuf.at[0, :, cols], first_sem.at[part]),
                pltpu.make_async_copy(rec.at[0, pl.ds(0, 2 * Q), later], rbuf.at[0, :, later], later_sem.at[part]))

    for part in range(PARTS):
        for copy in fetch(part):
            copy.start()
    flags = pltpu.make_async_copy(active_in, active, active_sem)
    flags.start()

    barrier = pltpu.get_barrier_semaphore()
    for i in range(1, WIN):
        pl.semaphore_signal(barrier, inc=1, device_id=peer(i), device_id_type=MESH)
    for dev in (at(-1, 0), at(1, 0), at(0, -1), at(0, 1), nxt, prv):
        pl.semaphore_signal(barrier, inc=1, device_id=dev, device_id_type=MESH)

    def against(table_rows, rows):
        return lax.dot_general(table_rows, rows, (((1,), (1,)), ((), ())), preferred_element_type=F32)

    def transform(sc):
        load(sc).wait()
        slot = sc % SLOTS_IN
        whiten(sc, against(tab[...], rbuf[slot, :, pl.ds(0, HALF)]), against(tab[...], rbuf[slot, :, pl.ds(HALF, HALF)]))

    def first_transform():
        acc[...] = jnp.zeros_like(acc)

        @pl.loop(0, PARTS)
        def _(part):
            for copy in fetch(part):
                copy.wait()
            cols = pl.ds(pl.multiple_of(part * PART_COLS, PART_COLS), PART_COLS)
            later = pl.ds(pl.multiple_of(HALF + part * PART_COLS, PART_COLS), PART_COLS)
            acc[0] += against(tab[:, cols], rbuf[0, :, cols])
            acc[1] += against(tab[:, cols], rbuf[0, :, later])

        for sc in range(1, SLOTS_IN):
            load(sc).start()
        whiten(0, acc[0], acc[1])

    def whiten(sc, early, later):
        odd = lax.broadcasted_iota(jnp.int32, early.shape, 0) % 2 == 1
        spectra = early + jnp.where(odd, -later, later)
        power = jnp.sum(spectra * spectra, axis=0, keepdims=True) / BINS
        white = (spectra * lax.rsqrt(power + EPSILON)).astype(BF16)
        for q in range(WIN):
            for ri in range(2):
                for qt in range(2):
                    wh[sc, q, qt, ri] = white[ri * BINS + q * BAND_BINS:ri * BINS + (q + 1) * BAND_BINS,
                                              qt * Q:(qt + 1) * Q]

        if isinstance(sc, int):
            load(sc + SLOTS_IN).start()
        else:
            @pl.when(sc + SLOTS_IN < 8)
            def _():
                load(sc + SLOTS_IN).start()

    def spread(sc, part=None):
        h, w = sc // LOCAL_W, sc % LOCAL_W
        row = pl.multiple_of((w * WIN + me) * BAND_BINS, BAND_BINS)

        @pl.loop(1, WIN)
        def _(i):
            to = peer(i)
            if part is None:
                src = wh.at[sc, to[0]]
                dst = blk.at[OWN, pl.ds(h * 2, 2), :, pl.ds(row, BAND_BINS), :]
            else:
                src = wh.at[sc, to[0], part // 2, part % 2]
                dst = blk.at[OWN, part // 2, part % 2, pl.ds(row, BAND_BINS), :]
            pltpu.make_async_remote_copy(
                src_ref=src, dst_ref=dst, send_sem=aa_send,
                recv_sem=aa_recv.at[sc if part is None else FIRST + part],
                device_id=to, device_id_type=MESH,
            ).start()

        for own in range(4) if part is None else (part,):
            blk[OWN, h * 2 + own // 2, own % 2, pl.ds(row, BAND_BINS), :] = wh[sc, me, own // 2, own % 2]

    def place(j):
        early = j < 16
        return jnp.where(early, j // 2 % 2, j // 8), jnp.where(early, j // 4, j // 2 % 4)

    def piece(block, j, two):
        quarter, w = place(j)
        return blk.at[block, quarter, slice(None) if two else j % 2, pl.ds(pl.multiple_of(w * 256, 256), 256), :]

    def z_sem(j, two):
        return z_recv.at[SINGLE // 2 + j // 2 if two else j]

    def wait_bytes(ref, sem):
        pltpu.make_async_copy(ref, ref, sem).wait()

    def send_z(j, two):
        pltpu.make_async_remote_copy(
            src_ref=piece(OWN, j, two), dst_ref=piece(UP4, j, two),
            send_sem=z_send, recv_sem=z_sem(j, two), device_id=at(-1, 0), device_id_type=MESH).start()

    def send_m(block, j, two):
        quarter, w = place(j)
        pltpu.make_async_remote_copy(
            src_ref=piece(block, j, two), dst_ref=piece(UP1, j, two),
            send_sem=m_send, recv_sem=m_recv.at[quarter * 4 + w], device_id=at(0, -1), device_id_type=MESH).start()

    def send_p(block, j, two):
        quarter, _ = place(j)
        pltpu.make_async_remote_copy(
            src_ref=piece(block, j, two), dst_ref=piece(UP3, j, two),
            send_sem=p_send, recv_sem=p_recv.at[quarter], device_id=at(0, 1), device_id_type=MESH).start()

    def send_on(j, two):
        wait_bytes(piece(UP4, j, two), z_sem(j, two))

        @pl.when((x <= 2) & (j < 24))
        def _():
            send_p(UP4, j, two)

        @pl.when(x == 0)
        def _():
            send_m(UP4, j, two)

    def send_own(j, two):
        send_z(j, two)

        @pl.when(x >= 1)
        def _():
            send_m(OWN, j, two)

        @pl.when((x == 3) & (j < 24))
        def _():
            send_p(OWN, j, two)

    def turn(left, quarter):
        block = jnp.where(left == 0, OWN, UP1)
        for ri in range(2):
            lt[left, ri, pl.ds(pl.multiple_of(quarter * Q, Q), Q), :] = blk[block, quarter, ri].T

    def products(left, rows, re, im, window=slice(None)):
        lre, lim = lt[left, 0, rows, window], lt[left, 1, rows, window]
        dot = functools.partial(jnp.dot, preferred_element_type=F32)
        real = dot(lre, re) + dot(lim, im)
        imag = dot(lim, re) - dot(lre, im)
        return real, imag

    def put_out(slot, rows, cols):
        pltpu.make_async_copy(ost.at[slot, :, rows, cols], out.at[slot, :, rows, cols], out_sem).start()

    def summary(slot, block, half, pair):
        rows = pl.ds(pl.multiple_of(half * 256, 256), 256)
        cols = pl.ds(pl.multiple_of(pair * 256, 256), 256)
        scale = active[0, slot].astype(F32) * (1.0 / math.sqrt(K))
        re, im = [jnp.concatenate([blk[block, pair * 2 + i, ri] for i in range(2)], axis=1) for ri in range(2)]
        real, imag = products(0, rows, re, im)
        ost[slot, 0, rows, cols] = (real * scale).astype(BF16)
        ost[slot, 1, rows, cols] = (imag * scale).astype(BF16)
        put_out(slot, rows, cols)

    def add_windows(w):
        window = pl.ds(pl.multiple_of(w * 256, 256), 256)
        wait_bytes(blk.at[UP3, 3, :, window, :], a2_recv.at[w])

        @pl.loop(0, 2)
        def _(half):
            rows = pl.ds(pl.multiple_of(half * 256, 256), 256)
            re, im = [jnp.concatenate([blk[UP3, c, ri, window, :] for c in (2, 3)], axis=1) for ri in range(2)]
            real, imag = products(0, rows, re, im, window)
            acc[0, rows, :] += real
            acc[1, rows, :] += imag

            @pl.when(w == 3)
            def _():
                for slot, c in ((3, 2), (2, 3)):
                    scale = active[0, slot].astype(F32) * (1.0 / math.sqrt(K))
                    cols = pl.ds(c * Q, Q)
                    ost[slot, :, rows, cols] = (acc[:, rows, (c - 2) * Q:(c - 1) * Q] * scale).astype(BF16)
                    put_out(slot, rows, cols)

    def tile_at(n):
        return (pick(n, {i: rc[0] for i, rc in enumerate(TILE_AT)}, 0),
                pick(n, {i: rc[1] for i, rc in enumerate(TILE_AT)}, 0))

    def ret_copy(n):
        sl = [
            (pl.ds(0, 2), slice(None), pl.ds(0, 256)),
            (pl.ds(2, 1), slice(None), pl.ds(0, 384)),
            (pl.ds(0, 2), slice(None), pl.ds(256, 128)),
            (pl.ds(3, 1), slice(None), pl.ds(0, 384)),
            (pl.ds(0, 2), slice(None), pl.ds(384, 128)),
            (pl.ds(2, 2), slice(None), pl.ds(384, 128)),
        ][n]
        return pltpu.make_async_remote_copy(
            src_ref=rp.at[sl], dst_ref=rv.at[sl],
            send_sem=ret_send, recv_sem=ret_recv.at[n], device_id=nxt, device_id_type=MESH)

    def give_back(rows, quarters):
        parts = [[blk[jnp.where(c == 3, UP4, UP3), c, ri] for c in quarters] for ri in range(2)]
        re, im = [p[0] if len(p) == 1 else jnp.concatenate(p, axis=1) for p in parts]
        scale = 1.0 / math.sqrt(K)
        for ri, product in enumerate(products(1, rows, re, im)):
            scaled = (product * scale).astype(BF16)
            for i, c in enumerate(quarters):
                rp[c, ri, rows, :] = scaled[:, i * Q:(i + 1) * Q]

    def take_back(n):
        r, c = tile_at(n)
        rows, cols = pl.ds(pl.multiple_of(r * Q, Q), Q), pl.ds(pl.multiple_of(c * Q, Q), Q)
        slot = jnp.where(c == 3, 3, 2)
        flag = active[0, slot].astype(F32)
        ost[slot, :, rows, cols] = (rv[c, :, rows, :].astype(F32) * flag).astype(BF16)
        put_out(slot, rows, cols)

    def when_in(k, table):
        def run(body):
            entries = {key: v if isinstance(v, tuple) else (v,) for key, v in table.items()}
            first = pick(k, {key: v[0] for key, v in entries.items()})

            @pl.when(first >= 0)
            def _():
                rest = [pick(k, {key: v[i] for key, v in entries.items()}, 0)
                        for i in range(1, len(next(iter(entries.values()))))]
                body(first, *rest)
        return run

    flags.wait()
    first_transform()
    pl.semaphore_wait(barrier, WIN - 1 + 6)
    for part in range(4):
        spread(0, part)
    acc[...] = jnp.zeros_like(acc)

    @pl.loop(0, LAST_STEP - FIRST_STEP + 1)
    def _(step):
        k = step + FIRST_STEP

        @pl.when((k >= 0) & (k < SINGLE))
        def _():
            send_on(k, False)

        @pl.when((k >= SINGLE) & (k < PIECES) & (k % 2 == 1))
        def _():
            send_on(k, True)

        @pl.when((k >= -SINGLE) & (k < 0))
        def _():
            wait_bytes(wh.at[0, pl.ds(0, WIN - 1), 0, 0], aa_recv.at[FIRST + 4 + k])
            send_own(k + SINGLE, False)

        @when_in(k, GATHERED)
        def _(sc):
            wait_bytes(wh.at[sc, pl.ds(0, WIN - 1)], aa_recv.at[sc])

        @pl.when((k >= 0) & (k + AHEAD < PIECES) & (k % 2 == 1))
        def _():
            send_own(k + AHEAD, True)

        @when_in(jnp.where((x == 1) | (x == 2), k + 2, k), FORWARD)
        def _(first, last):
            @pl.loop(first, last)
            def _(w):
                rows = pl.ds(pl.multiple_of(w * 256, 256), 256)
                wait_bytes(blk.at[UP1, 3, :, rows, :], m_recv.at[12 + w])
                pltpu.make_async_remote_copy(
                    src_ref=blk.at[UP1, 3, :, rows, :], dst_ref=blk.at[UP3, 3, :, rows, :],
                    send_sem=a2_send, recv_sem=a2_recv.at[w], device_id=prv, device_id_type=MESH).start()

        @when_in(k, TRANSFORM)
        def _(sc):
            transform(sc)

        @when_in(k, SPREAD)
        def _(sc):
            spread(sc)

        @when_in(k, WAIT_M)
        def _(first, last):
            @pl.loop(first * 4, last * 4)
            def _(i):
                rows = pl.ds(pl.multiple_of(i % 4 * 256, 256), 256)
                wait_bytes(blk.at[UP1, i // 4, :, rows, :], m_recv.at[i])

        @when_in(k, WAIT_P)
        def _(first, last):
            @pl.loop(first, last)
            def _(quarter):
                wait_bytes(blk.at[UP3, quarter], p_recv.at[quarter])

        @when_in(k, TURN)
        def _(left, first, last):
            @pl.loop(first, last)
            def _(quarter):
                turn(left, quarter)

        @when_in(k, BACK_HALF)
        def _(_):
            give_back(pl.ds(0, 256), (0, 1))

        @when_in(k, BACK_TALL)
        def _(quarter):
            give_back(pl.ds(0, 384), (quarter,))

        @when_in(k, BACK_WIDE)
        def _(quarter, pair):
            give_back(pl.ds(pl.multiple_of(quarter * Q, Q), Q), (pair * 2, pair * 2 + 1))

        for at_k, ns in RETURN.items():
            now = k == (at_k if ns != (0,) else jnp.where(x == 3, RETURN_EARLY, at_k))

            @pl.when(now)
            def _():
                for n in ns:
                    ret_copy(n).start()

        @when_in(k, SUMMARY)
        def _(slot, half, pair):
            block = pick(slot, {0: OWN, 1: UP1, 3: UP3, 4: UP4}, 0)
            summary(slot, block, half, pair)

        @when_in(k, PART)
        def _(w):
            add_windows(w)

        for at_k, ns in TAKE.items():
            @pl.when(k == at_k)
            def _():
                for n in ns:
                    ret_copy(n).wait_recv()

        tiles = {key: (TILES_OF[ns[0]][0], TILES_OF[ns[-1]][1]) for key, ns in TAKE.items()}

        @when_in(k, tiles)
        def _(first, last):
            @pl.loop(first, last)
            def _(n):
                take_back(n)

    wait_bytes(rp, ret_send)
    wait_bytes(blk.at[UP3, 3], a2_send)
    wait_bytes(blk.at[OWN], z_send)
    wait_bytes(blk.at[OWN], m_send)
    wait_bytes(blk.at[OWN, pl.ds(0, 3)], p_send)
    wait_bytes(wh.at[:, pl.ds(0, WIN - 1)], aa_send)
    pltpu.make_async_copy(ost, out, out_sem).wait()


def shards(records, active):
    dma = pltpu.SemaphoreType.DMA
    out = pl.pallas_call(
        kernel,
        out_shape=jax.ShapeDtypeStruct((SLOTS, 2, ST, ST), BF16),
        in_specs=[
            pl.BlockSpec(memory_space=pltpu.HBM),
            pl.BlockSpec(memory_space=pltpu.HBM),
            pl.BlockSpec(memory_space=pltpu.HBM),
        ],
        out_specs=pl.BlockSpec(memory_space=pl.ANY),
        scratch_shapes=[
            pltpu.SMEM((1, SLOTS), jnp.int32),
            pltpu.VMEM((2 * BINS, HALF), BF16),
            pltpu.VMEM((SLOTS_IN, 2 * Q, SAMPLES), BF16),
            pltpu.VMEM((8, WIN, 2, 2, BAND_BINS, Q), BF16),
            pltpu.VMEM((4, 4, 2, K, Q), BF16),
            pltpu.VMEM((2, 2, ST, K), BF16),
            pltpu.VMEM((4, 2, ST, Q), BF16),
            pltpu.VMEM((4, 2, ST, Q), BF16),
            pltpu.VMEM((SLOTS, 2, ST, ST), BF16),
            pltpu.VMEM((2, ST, 2 * Q), F32),
            dma((PARTS,)), dma((PARTS,)), dma((PARTS,)), dma((SLOTS_IN,)), dma, dma((FIRST + 4,)), dma, dma(((SINGLE + PIECES) // 2,)), dma, dma((16,)), dma, dma((3,)),
            dma, dma((4,)), dma, dma((6,)), dma, dma,
        ],
        compiler_params=pltpu.CompilerParams(
            collective_id=0, has_side_effects=True, vmem_limit_bytes=42 * 2**20),
        cost_estimate=pl.CostEstimate(flops=20 * 2**30, bytes_accessed=25 * 2**20, transcendentals=0),
    )(pltpu.with_memory_space_constraint(active, pltpu.HBM), records, pltpu.with_memory_space_constraint(jnp.asarray(spectral_table()), pltpu.HBM))
    return out.reshape(1, SLOTS, 1, 2 * ST, ST)


def solution(mesh):
    return jax.shard_map(
        shards,
        mesh=mesh,
        in_specs=(P("win", "blk", None), P("blk", None)),
        out_specs=P("blk", None, "win", None, None),
        check_vma=False,
    )
```
